128 devices in a mesh: row: 16 (over y, x), col: 8 (over z, core).
Axes of the slice: x: 4, y: 4, z: 4, core: 2. Of those that a mesh axis runs over, the one named last changes fastest.
Arguments:
- band_tiles: bfloat16 [16, 128, 256, 256], P('row', 'col'), may hold values from 0.0009994507 to 1
- band_cell: int32 [16, 128], P('row', 'col'), may hold values from 0 to 31, as said below
- band_count: int32 [16, 8], P('row', 'col'), may hold values from 1 to 16, as said below
- matrix_tiles: bfloat16 [16, 64, 256, 256], P('row', 'col'), may hold values from 7.390976e-05 to 0.07421875
- matrix_col: int32 [16, 64], P('row', 'col'), may hold values from 0 to 15
- matrix_live: int32 [16, 64], P('row', 'col'), may hold values 0 or 1
Outputs:
- reached: bfloat16 [8192, 32768], P('row', 'col')
- gained: float32 [], replicated
The draws below stay inside these ranges and needn't reach their ends.
Inputs may be any that keep to these rules, and one draw needn't show every extreme that they name: The band_cell values of one device's 16 slots are distinct. `band_count`: among the 8 devices of one index of row, the live slots with slot number 16 // 2 or more number at most 8 in all.
All inputs are finite; a program needn't handle non-finite values. No bound on the sum of `matrix_live` on one device may be relied on, other than what follows from the above.
Results may differ from the reference program's by a relative error of at most 0.001.
Values may be sent and summed in bfloat16 or wider, within the bound.
A program may use at most 128 MiB of HBM per device.

```python
import math
import jax
import jax.numpy as jnp
from jax import lax

TILE = 256
TILES = 128
BR = 2
BS = 16
KR = 8
N_ROW = 16
N_COL = 8


def draw_band_cell(key, part):
    keys = jax.random.split(jax.random.fold_in(key, 11), N_ROW * N_COL)

    def one_device(single):
        return jax.random.permutation(single, BR * (TILES // N_COL))[:BS].astype(jnp.int32)
    cells = jax.vmap(one_device)(keys)
    return cells.reshape(N_ROW, N_COL * BS)


def draw_band_count(key, part):
    half = BS // 2
    light = jax.random.randint(jax.random.fold_in(key, 21), (N_ROW, N_COL), 1, half + 1)
    first = jax.random.randint(jax.random.fold_in(key, 22), (N_ROW,), half + 1, BS + 1)
    second = half + (BS - first)
    keys = jax.random.split(jax.random.fold_in(key, 23), N_ROW)

    def one_row(single):
        return jax.random.permutation(single, N_COL)[:2].astype(jnp.int32)
    heavy = jax.vmap(one_row)(keys)
    columns = jnp.arange(N_COL, dtype=jnp.int32)[None, :]
    counts = jnp.where(columns == heavy[:, 0:1], first[:, None], light)
    counts = jnp.where(columns == heavy[:, 1:2], second[:, None], counts)
    return counts.astype(jnp.int32)


def plant(entries, own_key, smallest, high):
    longest = entries.shape.index(max(entries.shape))
    spots = []
    for shift in (0, 1):
        where = [jax.random.randint(jax.random.fold_in(own_key, axis), (), 0, length) for axis, length in enumerate(entries.shape)]
        where[longest] = (where[longest] + shift) % entries.shape[longest]
        spots.append(tuple(where))
    return entries.at[spots[0]].set(smallest).at[spots[1]].set(high)


def steps_of(stream_key, extent, pieces, least, top_value):
    factor_of = 1.0
    for dim, parts in pieces:
        steps = jax.random.uniform(jax.random.fold_in(jax.random.fold_in(stream_key, 6), dim), (parts,), jnp.float32, least / len(pieces), top_value / len(pieces))
        factor_of = factor_of * jnp.repeat(jnp.exp(steps), extent[dim] // parts).reshape((-1,) + (1,) * (len(extent) - 1 - dim))
    return factor_of


def setup_inputs(seed: int = 0) -> dict:
    seeds = jax.random.split(jax.random.key(seed), 7)
    return {
        "band_tiles": jnp.clip(jnp.exp(math.log(1.0) - 6.9083047 * jax.random.uniform(seeds[0], (N_ROW, N_COL * BS, TILE, TILE), jnp.float32) ** steps_of(seeds[0], (N_ROW, N_COL * BS, TILE, TILE), ((0, 16), (1, 8)), -0.2, 0.2)), 0.0009994507, 1.0).astype(jnp.bfloat16),
        "band_cell": draw_band_cell(jax.random.fold_in(seeds[6], 71), 0),
        "band_count": draw_band_count(jax.random.fold_in(seeds[6], 71), 0),
        "matrix_tiles": jnp.clip(jnp.exp(math.log(0.07421875) - 6.911927 * jax.random.uniform(seeds[3], (N_ROW, N_COL * KR, TILE, TILE), jnp.float32) ** steps_of(seeds[3], (N_ROW, N_COL * KR, TILE, TILE), ((0, 16), (1, 8)), -0.2, 0.2)), 7.390975952148438e-05, 0.07421875).astype(jnp.bfloat16),
        "matrix_col": plant(jax.random.randint(seeds[4], (N_ROW, N_COL * KR), 0, TILES // N_COL), jax.random.fold_in(seeds[4], 1), 0, (TILES // N_COL) - 1).astype(jnp.int32),
        "matrix_live": plant((jax.random.randint(seeds[5], (N_ROW, N_COL * KR), 0, 3) < 2).astype(jnp.int32), jax.random.fold_in(seeds[5], 1), 0, 1),
    }


def reference(band_tiles, band_cell, band_count, matrix_tiles, matrix_col, matrix_live):
    tcols = TILES // N_COL
    krows = TILES // N_ROW
    slots = N_COL * BS
    places = BR * tcols
    tiles_col = matrix_tiles.reshape(N_ROW, N_COL, krows, TILE, TILE)
    index_col = matrix_col.reshape(N_ROW, N_COL, krows)
    live_col = matrix_live.reshape(N_ROW, N_COL, krows)
    slot = jnp.arange(slots, dtype=jnp.int32)
    source = slot // BS
    spots = jnp.arange(places, dtype=jnp.int32)

    def one_block(index):
        rindex = index // N_COL
        cindex = index % N_COL
        a_tiles = band_tiles[rindex]
        a_cell = band_cell[rindex]
        a_count = band_count[rindex]
        valid = (slot % BS) < a_count[source]
        k_glob = source * tcols + a_cell % tcols
        i_loc = a_cell // tcols
        b_tiles = tiles_col[:, cindex].reshape(TILES, TILE, TILE)
        b_index = index_col[:, cindex].reshape(TILES)
        b_live = live_col[:, cindex].reshape(TILES)
        picked = jnp.take(b_tiles, k_glob, axis=0)
        live = (jnp.take(b_live, k_glob) > 0) & valid
        position = i_loc * tcols + jnp.take(b_index, k_glob)
        product = jnp.einsum("axy,ayz->axz", a_tiles.astype(jnp.float32), picked.astype(jnp.float32), precision=lax.Precision.HIGHEST)
        weights = ((position[:, None] == spots[None, :]) & live[:, None]).astype(jnp.float32)
        summed = jnp.einsum("ap,axz->pxz", weights, product, precision=lax.Precision.HIGHEST)
        own_start = (cindex * BS).astype(jnp.int32)
        own_tiles = lax.dynamic_slice_in_dim(a_tiles, own_start, BS, 0)
        own_cell = lax.dynamic_slice_in_dim(a_cell, own_start, BS, 0)
        own_live = jnp.arange(BS, dtype=jnp.int32) < a_count[cindex]
        own_w = ((own_cell[:, None] == spots[None, :]) & own_live[:, None]).astype(jnp.float32)
        base = jnp.einsum("sp,sxz->pxz", own_w, own_tiles.astype(jnp.float32), precision=lax.Precision.HIGHEST)
        expanded = jnp.minimum(1.0, base + summed)
        block = expanded.reshape(BR, tcols, TILE, TILE).transpose(0, 2, 1, 3).reshape(BR * TILE, tcols * TILE)
        return block.astype(jnp.bfloat16), jnp.sum(expanded - base)

    blocks, sums = lax.map(one_block, jnp.arange(N_ROW * N_COL, dtype=jnp.int32))
    reached = blocks.reshape(N_ROW, N_COL, BR * TILE, tcols * TILE).transpose(0, 2, 1, 3).reshape(N_ROW * BR * TILE, N_COL * tcols * TILE)
    gained = jnp.sum(sums) / (TILE * TILE * N_ROW * N_COL * BR * tcols)
    return reached, gained
```

```python
import functools

import jax
import jax.numpy as jnp
from jax import lax
from jax.experimental import pallas as pl
from jax.experimental.pallas import tpu as pltpu
from jax.sharding import PartitionSpec as P

TILE = 256
N_ROW, N_COL = 16, 8
SPOTS = 32
LOWER = 64
PRODUCTS = 72
ORDER = ((0, 0), (1, 0), (0, 1), (3, 0), (1, 1), (3, 1), (2, 0), (2, 1))
XA, XB, YA, YB = (0, 1), (0, 3), (1, 0), (3, 0)
MESH = pl.DeviceIdType.MESH


def tables(tab_v, enc_row, menc_row, y, x, col):
    shape = (128, 128)
    r = lax.broadcasted_iota(jnp.int32, shape, 0)
    l = lax.broadcasted_iota(jnp.int32, shape, 1)
    r1 = lax.broadcasted_iota(jnp.int32, (128, 1), 0)
    zero = jnp.zeros(shape, jnp.int32)
    eye = r == l

    def lanes(v):
        return jnp.sum(v, axis=1, keepdims=True)

    def to_row(column):
        return jnp.sum(jnp.where(eye, column + zero, 0), axis=0, keepdims=True)

    enc = enc_row + zero
    enc_col = lanes(jnp.where(eye, enc, 0))
    up_col = jnp.where(enc_col > 0, 1, 0) * ((r1 >> 3) & 1)
    rank_row = jnp.sum(jnp.where(r < l, up_col + zero, 0), axis=0, keepdims=True)
    up = jnp.where(enc > 0, 1, 0) * ((l >> 3) & 1)
    group = r1 >> 3
    source = jnp.zeros((128, 1), jnp.int32)
    for n, (dy, q) in enumerate(ORDER):
        source = jnp.where(group == n, ((y ^ dy) << 1) | ((x >> 1) ^ q), source)
    slot = (source << 4) + (r1 & 7)
    low_hit = jnp.where(l == slot + zero, 1, 0)
    up_hit = up * jnp.where(rank_row + zero == r - LOWER, 1, 0)
    pick = jnp.where(r < LOWER, low_hit, up_hit)
    cell_col = lanes(pick * enc)
    t_col = lanes(pick * l)
    cell = jnp.maximum(cell_col - 1, 0)
    kk, src = cell & 15, t_col >> 4
    menc_col = lanes(jnp.where(l == ((src << 4) + kk) + zero, menc_row + zero, 0))
    good = jnp.where(cell_col > 0, 1, 0) * jnp.where(menc_col > 0, 1, 0)
    pos_col = jnp.where(good > 0, ((cell >> 4) << 4) + menc_col - 1, -1)
    pos = pos_col + zero
    pos_row = to_row(pos_col)
    same = jnp.where(pos == pos_row + zero, 1, 0) * jnp.where(pos >= 0, 1, 0) * jnp.where(r < l, 1, 0)
    prev = jnp.max(jnp.where(same > 0, r, -1), axis=0, keepdims=True)
    last = jnp.max(jnp.where(pos == l, r, -1), axis=0, keepdims=True)
    own = jnp.where(enc_col + zero - 1 == l, 1, 0) * jnp.where((r >> 4) == col, 1, 0)
    base = jnp.max(jnp.where(own > 0, r & 15, -1), axis=0, keepdims=True)
    a_index = (((kk >> 3) ^ (x & 1)) << 3) | (kk & 7)
    tab_v[0:1, :] = to_row(a_index)
    tab_v[1:2, :] = jnp.where(prev < 0, PRODUCTS, prev)
    tab_v[2:3, :] = jnp.where(last < 0, PRODUCTS, last)
    tab_v[3:4, :] = jnp.where(base < 0, 16, base)
    tab_v[4:5, :] = to_row(((t_col >> 4) << 3) + (t_col & 7))
    tab_v[5:6, :] = to_row(src)
    tab_v[6:8, :] = jnp.zeros((2, 128), jnp.int32)


def kernel(
    cell_ref, count_ref, mcol_ref, mlive_ref, f_ref, a_ref, out_ref, gain_ref,
    a0, a1, a2, a3, a4, a5, a6, a7, fl, fu, fo, s_ref, picked, stage, mb, mm, tab_v, tab, gr, gc,
    a_send, a_recv, f_send, f_recv, m_send, m_recv, g_send, g_recv, local_sem, out_sem,
):
    row, col = lax.axis_index("row"), lax.axis_index("col")
    y, x, z, core = row >> 2, row & 3, col >> 1, col & 1
    groups = (a0, a1, a2, a3, a4, a5, a6, a7)

    barrier = pltpu.get_barrier_semaphore()
    for d in range(1, N_ROW):
        pl.semaphore_signal(barrier, inc=1, device_id=(row ^ d, col), device_id_type=MESH)
    for d in range(1, N_COL):
        pl.semaphore_signal(barrier, inc=1, device_id=(row, col ^ d), device_id_type=MESH)

    local = [
        pltpu.make_async_copy(a_ref, a0.at[pl.ds(0, 8)], local_sem.at[0]),
        pltpu.make_async_copy(f_ref.at[pl.ds(0, 8)], fl.at[pl.ds(col * 8, 8)], local_sem.at[1]),
        pltpu.make_async_copy(f_ref.at[pl.ds(8, 8)], fu.at[pl.ds(col * 8, 8)], local_sem.at[2]),
        pltpu.make_async_copy(f_ref, fo.at[pl.ds(0, 16)], local_sem.at[3]),
    ]
    for copy in local:
        copy.start()

    lane = lax.broadcasted_iota(jnp.int32, (8, 128), 1)
    own_b, own_m = jnp.zeros((8, 128), jnp.int32), jnp.zeros((8, 128), jnp.int32)
    for s in range(16):
        value = jnp.where(s < count_ref[0, 0], cell_ref[0, s] + 1, 0)
        own_b = jnp.where(lane == col * 16 + s, value, own_b)
    for s in range(8):
        value = jnp.where(mlive_ref[0, s] > 0, mcol_ref[0, s] + 1, 0)
        own_m = jnp.where(lane == row * 8 + s, value, own_m)
    mb[pl.ds(col, 1)] = own_b.reshape(1, 8, 128)
    mm[pl.ds(row, 1)] = own_m.reshape(1, 8, 128)

    pl.semaphore_wait(barrier, N_ROW + N_COL - 2)

    started = []

    def send(src, dst, send_sem, recv_sem, device):
        copy = pltpu.make_async_remote_copy(
            src_ref=src, dst_ref=dst, send_sem=send_sem, recv_sem=recv_sem,
            device_id=device, device_id_type=MESH,
        )
        copy.start()
        started.append(copy)

    def arrived(ref, sem):
        pltpu.make_async_remote_copy(
            src_ref=ref, dst_ref=ref, send_sem=m_send.at[0], recv_sem=sem,
            device_id=(row ^ 1, col), device_id_type=MESH,
        ).wait_recv()

    def a_block(dy, dx, q):
        return groups[dy * 2 + (dx >> 1)].at[pl.ds((dx & 1) * 8 + 2 * q, 2)]

    a_sent, a_here = [0], set()

    def a_wait(dy, dx, *quarters):
        for q in quarters:
            if (dy, dx) != (0, 0) and (dy, dx, q) not in a_here:
                a_here.add((dy, dx, q))
                arrived(a_block(dy, dx, q), a_recv.at[(dy * 4 + dx) * 4 + q])

    def a_send_to(link, dy, dx, *quarters):
        a_wait(dy, dx, *quarters)
        ly, lx = link
        to = ((y ^ ly) << 2) | (x ^ lx)
        for q in quarters:
            src = a_ref.at[pl.ds(2 * q, 2)] if (dy, dx) == (0, 0) else a_block(dy, dx, q)
            there = (dy ^ ly, dx ^ lx)
            send(
                src, a_block(*there, q), a_send.at[a_sent[0]],
                a_recv.at[(there[0] * 4 + there[1]) * 4 + q], (to, col),
            )
            a_sent[0] += 1

    def f_source(dz, dc):
        return ((z ^ dz) << 1) | (core ^ dc)

    def f_block(upper, source, h):
        return (fu if upper else fl).at[pl.ds(source * 8 + 4 * h, 4)]

    f_sent, f_here = [0], set()

    def f_wait(dz, dc, upper, h):
        if (dz, dc) != (0, 0) and (dz, dc, upper, h) not in f_here:
            f_here.add((dz, dc, upper, h))
            source = f_source(dz, dc)
            arrived(f_block(upper, source, h), f_recv.at[source * 4 + upper * 2 + h])

    def f_send_to(lz, lc, dz, upper, *halves):
        source = f_source(dz, 0)
        for h in halves:
            f_wait(dz, 0, upper, h)
            src = f_ref.at[pl.ds(8 * upper + 4 * h, 4)] if dz == 0 else f_block(upper, source, h)
            send(
                src, f_block(upper, source, h), f_send.at[f_sent[0]],
                f_recv.at[source * 4 + upper * 2 + h], (row, f_source(lz, lc)),
            )
            f_sent[0] += 1

    for d in range(1, N_COL):
        send(mb.at[pl.ds(col, 1)], mb.at[pl.ds(col, 1)], m_send.at[d], m_recv.at[col], (row, col ^ d))
    for d in range(1, N_ROW):
        send(mm.at[pl.ds(row, 1)], mm.at[pl.ds(row, 1)], m_send.at[8 + d], m_recv.at[8 + row], (row ^ d, col))
    for q in (0, 1):
        for link in (XA, XB):
            a_send_to(link, 0, 0, q)
        for link in (YA, YB):
            a_send_to(link, 0, 0, 2 + q)
        for lz in (1, 3):
            f_send_to(lz, 0, 0, 0, q)
    for q in (0, 1):
        for link in (XA, XB):
            a_send_to(link, 0, 0, 2 + q)
        for link in (YA, YB):
            a_send_to(link, 0, 0, q)
    f_send_to(0, 1, 0, 0, 0, 1)

    s_ref[PRODUCTS] = jnp.zeros((TILE, TILE), jnp.float32)
    fo[16] = jnp.zeros((TILE, TILE), jnp.bfloat16)
    for d in range(1, N_COL):
        arrived(mb.at[pl.ds(col ^ d, 1)], m_recv.at[col ^ d])
    for d in range(1, N_ROW):
        arrived(mm.at[pl.ds(row ^ d, 1)], m_recv.at[8 + (row ^ d)])
    enc_row = jnp.sum(mb[...], axis=0)[0:1, :]
    menc_row = jnp.sum(mm[...], axis=0)[0:1, :]
    tables(tab_v, enc_row, menc_row, y, x, col)
    to_scalars = pltpu.make_async_copy(tab_v, tab, local_sem.at[4])
    to_scalars.start()
    to_scalars.wait()

    def group_of(n):
        dy, q = ORDER[n]
        return groups[dy * 2 + q], ((y ^ dy) << 1) | ((x >> 1) ^ q)

    def products(n):
        a_group, source = group_of(n)
        for dx in (0, 1):
            a_wait(ORDER[n][0], 2 * ORDER[n][1] + dx, 0, 1, 2, 3)

        def lower(s, carry):
            o = n * 8 + s
            s_ref[o] = jnp.dot(
                fl[source * 8 + s], a_group[tab[0, o]], preferred_element_type=jnp.float32
            ) + s_ref[tab[1, o]]
            return carry

        lax.fori_loop(0, 8, lower, 0)

        def upper(j, carry):
            tile = a_group[tab[0, LOWER + j]]
            if n == 0:
                picked[j] = tile
            else:
                picked[j] = jnp.where(tab[5, LOWER + j] == source, tile, picked[j])
            return carry

        lax.fori_loop(0, 8, upper, 0)

    f_send_to(1, 0, 3, 0, 0)
    f_send_to(3, 0, 1, 0, 1)
    for h in (0, 1):
        for lz in (1, 3):
            f_send_to(lz, 0, 0, 1, h)
    a_send_to(XA, 0, 3, 0)
    a_send_to(XB, 0, 1, 1)
    a_send_to(YA, 3, 0, 2)
    a_send_to(YB, 1, 0, 3)
    for dx in (1, 3):
        for link in (YA, YB):
            a_send_to(link, 0, dx, 0, 1)
        for link in (XA, XB):
            a_send_to(link, dx, 0, 2, 3)
    f_send_to(0, 1, 1, 0, 0, 1)
    f_send_to(0, 1, 3, 0, 0, 1)
    f_send_to(0, 1, 0, 1, 0, 1)
    a_send_to(XA, 0, 3, 2)
    a_send_to(XB, 0, 1, 3)
    for link in (YA, YB):
        a_send_to(link, 0, 2, 0, 1)
    for link in (XA, XB):
        a_send_to(link, 2, 0, 2, 3)
    f_send_to(0, 1, 2, 0, 0, 1)
    f_send_to(1, 0, 3, 1, 0)
    f_send_to(3, 0, 1, 1, 1)
    a_send_to(YA, 3, 0, 0)
    a_send_to(YB, 1, 0, 1)
    a_send_to(XA, 1, 3, 2)
    a_send_to(XB, 1, 1, 3)
    for d in (1, 3):
        a_send_to(YA, 3, d, 0)
        a_send_to(YB, 1, d, 1)
    a_send_to(XA, 3, 3, 2)
    a_send_to(XB, 3, 1, 3)
    a_send_to(YA, 3, 2, 0)
    a_send_to(YB, 1, 2, 1)
    a_send_to(XA, 2, 3, 2)
    a_send_to(XB, 2, 1, 3)
    f_send_to(0, 1, 1, 1, 0, 1)
    f_send_to(0, 1, 3, 1, 0, 1)
    f_send_to(0, 1, 2, 1, 0, 1)

    for copy in local:
        copy.wait()
    for dz in range(4):
        for h in (0, 1):
            f_wait(dz, 1, 0, h)
    for n in range(8):
        products(n)
    for dz in range(4):
        for h in (0, 1):
            f_wait(dz, 1, 1, h)

    def spilled(j, carry):
        o = LOWER + j
        s_ref[o] = jnp.dot(
            fu[tab[4, o]], picked[j], preferred_element_type=jnp.float32
        ) + s_ref[tab[1, o]]
        return carry

    lax.fori_loop(0, 8, spilled, 0)

    outs = []
    total = jnp.zeros((8, TILE), jnp.float32)
    for i in range(2):

        def output(c, total):
            base = fo[tab[3, i * 16 + c]].astype(jnp.float32)
            full = jnp.minimum(1.0, base + s_ref[tab[2, i * 16 + c]])
            stage[pl.ds(i * TILE, TILE), pl.ds(pl.multiple_of(c * TILE, TILE), TILE)] = full.astype(jnp.bfloat16)
            return total + jnp.sum((full - base).reshape(TILE // 8, 8, TILE), axis=0)

        total = lax.fori_loop(0, 16, output, total)
        rows = pl.ds(i * TILE, TILE)
        copy = pltpu.make_async_copy(stage.at[rows], out_ref.at[rows], out_sem.at[i])
        copy.start()
        outs.append(copy)

    gr[pl.ds(row, 1)] = (total[:, :128] + total[:, 128:]).reshape(1, 8, 128)
    for d in range(1, N_ROW):
        send(gr.at[pl.ds(row, 1)], gr.at[pl.ds(row, 1)], g_send.at[d], g_recv.at[row], (row ^ d, col))
    for d in range(1, N_ROW):
        arrived(gr.at[pl.ds(row ^ d, 1)], g_recv.at[row ^ d])
    gc[pl.ds(col, 1)] = jnp.sum(gr[...], axis=0).reshape(1, 8, 128)
    for d in range(1, N_COL):
        send(gc.at[pl.ds(col, 1)], gc.at[pl.ds(col, 1)], g_send.at[16 + d], g_recv.at[16 + col], (row, col ^ d))
    for d in range(1, N_COL):
        arrived(gc.at[pl.ds(col ^ d, 1)], g_recv.at[16 + (col ^ d)])
    gain_ref[...] = jnp.sum(gc[...], axis=0)
    for copy in started:
        copy.wait_send()
    for copy in outs:
        copy.wait()


def on_device(band_tiles, band_cell, band_count, matrix_tiles, matrix_col, matrix_live):
    smem = pl.BlockSpec(memory_space=pltpu.SMEM)
    hbm = pl.BlockSpec(memory_space=pl.ANY)
    tiles = (TILE, TILE)
    reached, gain = pl.pallas_call(
        kernel,
        out_shape=(
            jax.ShapeDtypeStruct((2 * TILE, 16 * TILE), jnp.bfloat16),
            jax.ShapeDtypeStruct((8, 128), jnp.float32),
        ),
        in_specs=[smem] * 4 + [hbm] * 2,
        out_specs=(hbm, pl.BlockSpec(memory_space=pltpu.VMEM)),
        scratch_shapes=[pltpu.VMEM((16, *tiles), jnp.bfloat16)] * 8
        + [
            pltpu.VMEM((LOWER, *tiles), jnp.bfloat16),
            pltpu.VMEM((LOWER, *tiles), jnp.bfloat16),
            pltpu.VMEM((17, *tiles), jnp.bfloat16),
            pltpu.VMEM((PRODUCTS + 1, *tiles), jnp.float32),
            pltpu.VMEM((8, *tiles), jnp.bfloat16),
            pltpu.VMEM((2 * TILE, 16 * TILE), jnp.bfloat16),
            pltpu.VMEM((N_COL, 8, 128), jnp.int32),
            pltpu.VMEM((N_ROW, 8, 128), jnp.int32),
            pltpu.VMEM((8, 128), jnp.int32),
            pltpu.SMEM((8, 128), jnp.int32),
            pltpu.VMEM((N_ROW, 8, 128), jnp.float32),
            pltpu.VMEM((N_COL, 8, 128), jnp.float32),
            pltpu.SemaphoreType.DMA((60,)),
            pltpu.SemaphoreType.DMA((64,)),
            pltpu.SemaphoreType.DMA((28,)),
            pltpu.SemaphoreType.DMA((32,)),
            pltpu.SemaphoreType.DMA((24,)),
            pltpu.SemaphoreType.DMA((24,)),
            pltpu.SemaphoreType.DMA((24,)),
            pltpu.SemaphoreType.DMA((24,)),
            pltpu.SemaphoreType.DMA((5,)),
            pltpu.SemaphoreType.DMA((2,)),
        ],
        compiler_params=pltpu.CompilerParams(
            collective_id=0, has_side_effects=True, vmem_limit_bytes=60 * 1024 * 1024
        ),
    )(band_cell, band_count, matrix_col, matrix_live, band_tiles[0], matrix_tiles[0])
    return reached, jnp.sum(gain) / 268435456.0


def solution(mesh):
    placed = P("row", "col")
    tiled = P("row", "col", None, None)
    return jax.shard_map(
        on_device, mesh=mesh,
        in_specs=(tiled, placed, placed, tiled, placed, placed),
        out_specs=(placed, P()), check_vma=False,
    )
```

```python
import functools

import jax
import jax.numpy as jnp
from jax import lax
from jax.experimental import pallas as pl
from jax.experimental.pallas import tpu as pltpu
from jax.sharding import PartitionSpec as P

TILE = 256
N_ROW, N_COL = 16, 8
SPOTS = 32
LOWER = 64
PRODUCTS = 72
ORDER = ((0, 0), (1, 0), (3, 0), (0, 1), (1, 1), (2, 0), (3, 1), (2, 1))
UNROLL = 4
DEPTH = 2
XA, XB, YA, YB = (0, 1), (0, 3), (1, 0), (3, 0)
NEAR_ROW, NEAR_COL = (1, 3, 4, 12), (2, 6, 1)
MESH = pl.DeviceIdType.MESH


def tables(tab_v, enc_row, menc_row, y, x, col):
    shape = (128, 128)
    r = lax.broadcasted_iota(jnp.int32, shape, 0)
    l = lax.broadcasted_iota(jnp.int32, shape, 1)
    r1 = lax.broadcasted_iota(jnp.int32, (128, 1), 0)
    zero = jnp.zeros(shape, jnp.int32)
    eye = r == l

    def lanes(v):
        return jnp.sum(v, axis=1, keepdims=True)

    def to_row(column):
        return jnp.sum(jnp.where(eye, column + zero, 0), axis=0, keepdims=True)

    enc = enc_row + zero
    enc_col = lanes(jnp.where(eye, enc, 0))
    up_col = jnp.where(enc_col > 0, 1, 0) * ((r1 >> 3) & 1)
    rank_row = jnp.sum(jnp.where(r < l, up_col + zero, 0), axis=0, keepdims=True)
    up = jnp.where(enc > 0, 1, 0) * ((l >> 3) & 1)
    group = r1 >> 3
    source = jnp.zeros((128, 1), jnp.int32)
    for n, (dy, q) in enumerate(ORDER):
        source = jnp.where(group == n, ((y ^ dy) << 1) | ((x >> 1) ^ q), source)
    slot = (source << 4) + (r1 & 7)
    low_hit = jnp.where(l == slot + zero, 1, 0)
    up_hit = up * jnp.where(rank_row + zero == r - LOWER, 1, 0)
    pick = jnp.where(r < LOWER, low_hit, up_hit)
    cell_col = lanes(pick * enc)
    t_col = lanes(pick * l)
    cell = jnp.maximum(cell_col - 1, 0)
    kk, src = cell & 15, t_col >> 4
    menc_col = lanes(jnp.where(l == ((src << 4) + kk) + zero, menc_row + zero, 0))
    good = jnp.where(cell_col > 0, 1, 0) * jnp.where(menc_col > 0, 1, 0)
    pos_col = jnp.where(good > 0, ((cell >> 4) << 4) + menc_col - 1, -1)
    pos = pos_col + zero
    pos_row = to_row(pos_col)
    same = jnp.where(pos == pos_row + zero, 1, 0) * jnp.where(pos >= 0, 1, 0) * jnp.where(r < l, 1, 0)
    prev = jnp.max(jnp.where(same > 0, r, -1), axis=0, keepdims=True)
    last = jnp.max(jnp.where(pos == l, r, -1), axis=0, keepdims=True)
    own = jnp.where(enc_col + zero - 1 == l, 1, 0) * jnp.where((r >> 4) == col, 1, 0)
    base = jnp.max(jnp.where(own > 0, r & 15, -1), axis=0, keepdims=True)
    a_index = (((kk >> 3) ^ (x & 1)) << 3) | (kk & 7)
    tab_v[0:1, :] = to_row(a_index)
    tab_v[1:2, :] = jnp.where(prev < 0, PRODUCTS, prev)
    tab_v[2:3, :] = jnp.where(last < 0, PRODUCTS, last)
    tab_v[3:4, :] = jnp.where(base < 0, 16, base)
    tab_v[4:5, :] = to_row(((t_col >> 4) << 3) + (t_col & 7))
    tab_v[5:6, :] = to_row(src)
    tab_v[6:8, :] = jnp.zeros((2, 128), jnp.int32)


def kernel(
    cell_in, count_in, mcol_in, mlive_in, f_ref, a_ref, out_ref, gain_ref,
    cell_ref, count_ref, mcol_ref, mlive_ref,
    a0, a1, a2, a3, a4, a5, a6, a7, fl, fu, fo, s_ref, picked, stage, mb, mm, mb_in, mm_in, tab_v, tab, gains,
    a_send, a_recv, f_send, f_recv, m_send, m_recv, g_send, g_recv, local_sem, out_sem,
):
    row, col = lax.axis_index("row"), lax.axis_index("col")
    y, x, z, core = row >> 2, row & 3, col >> 1, col & 1
    groups = (a0, a1, a2, a3, a4, a5, a6, a7)

    barrier = pltpu.get_barrier_semaphore()
    for d in NEAR_ROW:
        pl.semaphore_signal(barrier, inc=1, device_id=(row ^ d, col), device_id_type=MESH)
    for d in NEAR_COL:
        pl.semaphore_signal(barrier, inc=1, device_id=(row, col ^ d), device_id_type=MESH)

    scalars = [
        pltpu.make_async_copy(there, here, local_sem.at[5 + i])
        for i, (there, here) in enumerate(
            ((cell_in, cell_ref), (count_in, count_ref), (mcol_in, mcol_ref), (mlive_in, mlive_ref))
        )
    ]
    for copy in scalars:
        copy.start()
    local = [
        pltpu.make_async_copy(a_ref, a0.at[pl.ds(0, 8)], local_sem.at[0]),
        pltpu.make_async_copy(f_ref.at[pl.ds(0, 8)], fl.at[pl.ds(col * 8, 8)], local_sem.at[1]),
        pltpu.make_async_copy(f_ref.at[pl.ds(8, 8)], fu.at[pl.ds(col * 8, 8)], local_sem.at[2]),
        pltpu.make_async_copy(f_ref, fo.at[pl.ds(0, 16)], local_sem.at[3]),
    ]
    for copy in local:
        copy.start()

    pl.semaphore_wait(barrier, len(NEAR_ROW) + len(NEAR_COL))

    started = []

    def send(src, dst, send_sem, recv_sem, device, keep=True):
        copy = pltpu.make_async_remote_copy(
            src_ref=src, dst_ref=dst, send_sem=send_sem, recv_sem=recv_sem,
            device_id=device, device_id_type=MESH,
        )
        copy.start()
        if keep:
            started.append(copy)
        return copy

    def arrived(ref, sem):
        pltpu.make_async_remote_copy(
            src_ref=ref, dst_ref=ref, send_sem=m_send.at[0], recv_sem=sem,
            device_id=(row ^ 1, col), device_id_type=MESH,
        ).wait_recv()

    def a_block(dy, dx, q):
        return groups[dy * 2 + (dx >> 1)].at[pl.ds((dx & 1) * 8 + 2 * q, 2)]

    a_here, f_here = set(), set()

    def a_wait(dy, dx, *quarters):
        for q in quarters:
            if (dy, dx) != (0, 0) and (dy, dx, q) not in a_here:
                a_here.add((dy, dx, q))
                arrived(a_block(dy, dx, q), a_recv.at[(dy * 4 + dx) * 4 + q])

    def f_source(dz, dc):
        return ((z ^ dz) << 1) | (core ^ dc)

    def f_block(dz, dc, u, n=2):
        upper, first = u // 4, 2 * (u % 4)
        return (fu if upper else fl).at[pl.ds(f_source(dz, dc) * 8 + first, n)]

    def f_wait(dz, *units):
        for u in units:
            if dz and (dz, u) not in f_here:
                f_here.add((dz, u))
                arrived(f_block(dz, 0, u), f_recv.at[dz * 8 + u])

    def sib_wait(upper):
        for dz in range(4):
            for u in (4 * upper, 4 * upper + 2):
                arrived(f_block(dz, 1, u, 4), f_recv.at[32 + dz * 4 + u // 2])

    def sib_send(dz, *halves):
        for h in halves:
            f_wait(dz, 2 * h, 2 * h + 1)
            src = f_ref.at[pl.ds(4 * h, 4)] if dz == 0 else f_block(dz, 0, 2 * h, 4)
            send(
                src, f_block(dz, 0, 2 * h, 4), f_send.at[24 + dz * 4 + h],
                f_recv.at[32 + dz * 4 + h], (row, col ^ 1),
            )

    def x_link(near, part):
        turn = [((0, 0), 0), ((0, 0), 1), ((0, 0), 2), ((0, near), part), ((0, 0), 3)]
        turn += [((dy, 0), q) for dy in (1, 3, 2) for q in (2, 3)]
        return turn + [((dy, near), part + 2) for dy in (0, 1, 3, 2)]

    def y_link(near, part):
        turn = [((0, 0), 2), ((0, 0), 3), ((0, 0), 0), ((near, 0), part + 2), ((0, 0), 1)]
        turn += [((0, dx), q) for dx in (1, 3, 2) for q in (0, 1)]
        return turn + [((near, dx), part) for dx in (0, 1, 3, 2)]

    def z_link(near, part):
        turn = [(0, u) for u in range(4)] + [(near, 2 * part), (near, 2 * part + 1)]
        return turn + [(0, u) for u in range(4, 8)] + [(near, 4 + 2 * part), (near, 5 + 2 * part)]

    a_links = ((XA, x_link(3, 0)), (YA, y_link(3, 0)), (XB, x_link(1, 1)), (YB, y_link(1, 1)))
    z_links = ((1, z_link(3, 0)), (3, z_link(1, 1)))
    flying = {}

    def pace(link):
        queue = flying.setdefault(link, [])
        if len(queue) == DEPTH:
            queue.pop(0).wait_send()
        return queue

    def turn(k):
        for i, ((ly, lx), order) in enumerate(a_links):
            (dy, dx), q = order[k]
            queue = pace(i)
            a_wait(dy, dx, q)
            src = a_ref.at[pl.ds(2 * q, 2)] if (dy, dx) == (0, 0) else a_block(dy, dx, q)
            there = (dy ^ ly, dx ^ lx)
            queue.append(send(
                src, a_block(*there, q), a_send.at[i * 15 + k],
                a_recv.at[(there[0] * 4 + there[1]) * 4 + q],
                (((y ^ ly) << 2) | (x ^ lx), col), False,
            ))
        if k < 12:
            for i, (lz, order) in enumerate(z_links):
                dz, u = order[k]
                queue = pace(4 + i)
                f_wait(dz, u)
                src = f_ref.at[pl.ds(2 * u, 2)] if dz == 0 else f_block(dz, 0, u)
                queue.append(send(
                    src, f_block(dz, 0, u), f_send.at[i * 12 + k],
                    f_recv.at[(dz ^ lz) * 8 + u], (row, f_source(lz, 0)), False,
                ))

    def own_rows():
        for copy in scalars:
            copy.wait()
        lane = lax.broadcasted_iota(jnp.int32, (8, 128), 1)
        own_b, own_m = jnp.zeros((8, 128), jnp.int32), jnp.zeros((8, 128), jnp.int32)
        for s in range(16):
            value = jnp.where(s < count_ref[0, 0], cell_ref[0, s] + 1, 0)
            own_b = jnp.where(lane == col * 16 + s, value, own_b)
        for s in range(8):
            value = jnp.where(mlive_ref[0, s] > 0, mcol_ref[0, s] + 1, 0)
            own_m = jnp.where(lane == row * 8 + s, value, own_m)
        mb[0] = own_b
        mm[0] = own_m

    def m_exchange(k):
        if k < 4:
            send(mm.at[k], mm_in.at[k], m_send.at[k], m_recv.at[k], (row ^ NEAR_ROW[k], col))
        if k < 3:
            send(mb.at[k], mb_in.at[k], m_send.at[4 + k], m_recv.at[4 + k], (row, col ^ NEAR_COL[k]))

    def m_add(k):
        if k < 4:
            arrived(mm_in.at[k], m_recv.at[k])
            mm[k + 1] = mm[k] + mm_in[k]
        if k < 3:
            arrived(mb_in.at[k], m_recv.at[4 + k])
            mb[k + 1] = mb[k] + mb_in[k]

    s_ref[PRODUCTS] = jnp.zeros((TILE, TILE), jnp.float32)
    fo[16] = jnp.zeros((TILE, TILE), jnp.bfloat16)

    def group_of(n):
        dy, q = ORDER[n]
        return groups[dy * 2 + q], ((y ^ dy) << 1) | ((x >> 1) ^ q)

    def products(n):
        a_group, source = group_of(n)
        for dx in (0, 1):
            a_wait(ORDER[n][0], 2 * ORDER[n][1] + dx, 0, 1, 2, 3)

        def lower(s, carry):
            o = n * 8 + s
            s_ref[o] = jnp.dot(
                fl[source * 8 + s], a_group[tab[0, o]], preferred_element_type=jnp.float32
            ) + s_ref[tab[1, o]]
            return carry

        lax.fori_loop(0, 8, lower, 0, unroll=UNROLL)

        def upper(j, carry):
            tile = a_group[tab[0, LOWER + j]]
            if n == 0:
                picked[j] = tile
            else:
                picked[j] = jnp.where(tab[5, LOWER + j] == source, tile, picked[j])
            return carry

        lax.fori_loop(0, 8, upper, 0)

    for k in range(15):
        turn(k)
        if k == 0:
            own_rows()
            m_exchange(0)
        if k in (1, 3, 5):
            m_add(k // 2)
            m_exchange(k // 2 + 1)
        if k == 2:
            sib_send(0, 0, 1, 2, 3)
        if k == 6:
            sib_send(1, 0, 1)
            sib_send(3, 0, 1)
        if k == 7:
            m_add(3)
            tables(tab_v, mb[3, 0:1, :], mm[4, 0:1, :], y, x, col)
            to_scalars = pltpu.make_async_copy(tab_v, tab, local_sem.at[4])
            to_scalars.start()
            to_scalars.wait()
        if k == 8:
            sib_send(2, 0, 1)
        if k == 10:
            for copy in local:
                copy.wait()
            sib_wait(0)
            products(0)
        if k == 11:
            products(1)
            products(2)
        if k == 12:
            sib_send(1, 2, 3)
            sib_send(3, 2, 3)
        if k == 13:
            products(3)
    sib_send(2, 2, 3)
    for n in range(4, 8):
        products(n)
    sib_wait(1)

    def spilled(j, carry):
        o = LOWER + j
        s_ref[o] = jnp.dot(
            fu[tab[4, o]], picked[j], preferred_element_type=jnp.float32
        ) + s_ref[tab[1, o]]
        return carry

    lax.fori_loop(0, 8, spilled, 0, unroll=UNROLL)

    outs = []
    total = jnp.zeros((8, TILE), jnp.float32)
    for i in range(2):

        def output(c, total):
            base = fo[tab[3, i * 16 + c]].astype(jnp.float32)
            full = jnp.minimum(1.0, base + s_ref[tab[2, i * 16 + c]])
            stage[pl.ds(i * TILE, TILE), pl.ds(pl.multiple_of(c * TILE, TILE), TILE)] = full.astype(jnp.bfloat16)
            return total + jnp.sum((full - base).reshape(TILE // 8, 8, TILE), axis=0)

        total = lax.fori_loop(0, 16, output, total, unroll=2)
        rows = pl.ds(i * TILE, TILE)
        copy = pltpu.make_async_copy(stage.at[rows], out_ref.at[rows], out_sem.at[i])
        copy.start()
        outs.append(copy)

    part = total[:, :128] + total[:, 128:]
    for k, n in enumerate((N_ROW, N_COL)):
        gains[k, 0] = part
        for d in range(1, n):
            device = (row, col ^ d) if k else (row ^ d, col)
            send(gains.at[k, 0], gains.at[k, d], g_send.at[k * N_ROW + d], g_recv.at[k], device)
        arrived(gains.at[k, pl.ds(1, n - 1)], g_recv.at[k])
        parts = [gains[k, d] for d in range(n)]
        while len(parts) > 1:
            parts = [parts[2 * i] + parts[2 * i + 1] for i in range(len(parts) // 2)]
        part = parts[0]
    gain_ref[0, 0] = jnp.sum(part) * (1.0 / 268435456.0)
    for queue in flying.values():
        started.extend(queue)
    for copy in started:
        copy.wait_send()
    for copy in outs:
        copy.wait()


def store_kernel(from_ref, to_ref, held, sem_in, sem_out):
    rows = [pl.ds(64 * i, 64) for i in range(8)]
    ins = [pltpu.make_async_copy(from_ref.at[r], held.at[r], sem_in.at[i]) for i, r in enumerate(rows)]
    outs = [pltpu.make_async_copy(held.at[r], to_ref.at[r], sem_out.at[i]) for i, r in enumerate(rows)]
    for copy in ins:
        copy.start()
    for into, out in zip(ins, outs):
        into.wait()
        out.start()
    for copy in outs:
        copy.wait()


def on_device(band_tiles, band_cell, band_count, matrix_tiles, matrix_col, matrix_live):
    smem = pl.BlockSpec(memory_space=pltpu.SMEM)
    hbm = pl.BlockSpec(memory_space=pl.ANY)
    tiles = (TILE, TILE)
    reached, gain = pl.pallas_call(
        kernel,
        out_shape=(
            jax.ShapeDtypeStruct((2 * TILE, 16 * TILE), jnp.bfloat16),
            jax.ShapeDtypeStruct((1, 1), jnp.float32),
        ),
        in_specs=[hbm] * 6,
        out_specs=(hbm, smem),
        scratch_shapes=[pltpu.SMEM((1, n), jnp.int32) for n in (16, 1, 8, 8)]
        + [pltpu.VMEM((16, *tiles), jnp.bfloat16)] * 8
        + [
            pltpu.VMEM((LOWER, *tiles), jnp.bfloat16),
            pltpu.VMEM((LOWER, *tiles), jnp.bfloat16),
            pltpu.VMEM((17, *tiles), jnp.bfloat16),
            pltpu.VMEM((PRODUCTS + 1, *tiles), jnp.float32),
            pltpu.VMEM((8, *tiles), jnp.bfloat16),
            pltpu.VMEM((2 * TILE, 16 * TILE), jnp.bfloat16),
            pltpu.VMEM((4, 8, 128), jnp.int32),
            pltpu.VMEM((5, 8, 128), jnp.int32),
            pltpu.VMEM((3, 8, 128), jnp.int32),
            pltpu.VMEM((4, 8, 128), jnp.int32),
            pltpu.VMEM((8, 128), jnp.int32),
            pltpu.SMEM((8, 128), jnp.int32),
            pltpu.VMEM((2, N_ROW, 8, 128), jnp.float32),
            pltpu.SemaphoreType.DMA((60,)),
            pltpu.SemaphoreType.DMA((64,)),
            pltpu.SemaphoreType.DMA((40,)),
            pltpu.SemaphoreType.DMA((48,)),
            pltpu.SemaphoreType.DMA((7,)),
            pltpu.SemaphoreType.DMA((7,)),
            pltpu.SemaphoreType.DMA((24,)),
            pltpu.SemaphoreType.DMA((2,)),
            pltpu.SemaphoreType.DMA((9,)),
            pltpu.SemaphoreType.DMA((2,)),
        ],
        compiler_params=pltpu.CompilerParams(
            collective_id=0, has_side_effects=True, vmem_limit_bytes=60 * 1024 * 1024
        ),
    )(band_cell, band_count, matrix_col, matrix_live, band_tiles[0], matrix_tiles[0])
    reached = pl.pallas_call(
        store_kernel,
        out_shape=jax.ShapeDtypeStruct((2 * TILE, 16 * TILE), jnp.bfloat16),
        in_specs=[hbm],
        out_specs=hbm,
        scratch_shapes=[
            pltpu.VMEM((2 * TILE, 16 * TILE), jnp.bfloat16),
            pltpu.SemaphoreType.DMA((8,)),
            pltpu.SemaphoreType.DMA((8,)),
        ],
        compiler_params=pltpu.CompilerParams(vmem_limit_bytes=60 * 1024 * 1024),
    )(reached)
    return reached, gain.reshape(())


def solution(mesh):
    placed = P("row", "col")
    tiled = P("row", "col", None, None)
    return jax.shard_map(
        on_device, mesh=mesh,
        in_specs=(tiled, placed, placed, tiled, placed, placed),
        out_specs=(placed, P()), check_vma=False,
    )
```

```python
import functools

import jax
import jax.numpy as jnp
from jax import lax
from jax.experimental import pallas as pl
from jax.experimental.pallas import tpu as pltpu
from jax.sharding import PartitionSpec as P

TILE = 256
N_ROW, N_COL = 16, 8
SPOTS = 32
LOWER = 64
PRODUCTS = 72
BLANK = PRODUCTS + 16
ORDER = ((0, 0), (1, 0), (3, 0), (0, 1), (1, 1), (2, 0), (3, 1), (2, 1))
UNROLL = 8
DEPTH = 2
XA, XB, YA, YB = (0, 1), (0, 3), (1, 0), (3, 0)
NEAR_ROW, NEAR_COL = (1, 3, 4, 12), (2, 6, 1)
FAR_FIRST = (10, 9, 11, 6, 14, 2, 8, 5, 7, 13, 15, 1, 3, 4, 12)
MESH = pl.DeviceIdType.MESH


def tables(tab_v, enc_row, menc_row, y, x, col):
    shape = (128, 128)
    r = lax.broadcasted_iota(jnp.int32, shape, 0)
    l = lax.broadcasted_iota(jnp.int32, shape, 1)
    r1 = lax.broadcasted_iota(jnp.int32, (128, 1), 0)
    zero = jnp.zeros(shape, jnp.int32)
    eye = r == l

    def lanes(v):
        return jnp.sum(v, axis=1, keepdims=True)

    def to_row(column):
        return jnp.sum(jnp.where(eye, column + zero, 0), axis=0, keepdims=True)

    enc = enc_row + zero
    enc_col = lanes(jnp.where(eye, enc, 0))
    up_col = jnp.where(enc_col > 0, 1, 0) * ((r1 >> 3) & 1)
    rank_row = jnp.sum(jnp.where(r < l, up_col + zero, 0), axis=0, keepdims=True)
    up = jnp.where(enc > 0, 1, 0) * ((l >> 3) & 1)
    group = r1 >> 3
    source = jnp.zeros((128, 1), jnp.int32)
    for n, (dy, q) in enumerate(ORDER):
        source = jnp.where(group == n, ((y ^ dy) << 1) | ((x >> 1) ^ q), source)
    slot = (source << 4) + (r1 & 7)
    low_hit = jnp.where(l == slot + zero, 1, 0)
    up_hit = up * jnp.where(rank_row + zero == r - LOWER, 1, 0)
    pick = jnp.where(r < LOWER, low_hit, up_hit)
    cell_col = lanes(pick * enc)
    t_col = lanes(pick * l)
    cell = jnp.maximum(cell_col - 1, 0)
    kk, src = cell & 15, t_col >> 4
    menc_col = lanes(jnp.where(l == ((src << 4) + kk) + zero, menc_row + zero, 0))
    good = jnp.where(cell_col > 0, 1, 0) * jnp.where(menc_col > 0, 1, 0)
    pos_col = jnp.where(good > 0, ((cell >> 4) << 4) + menc_col - 1, -1)
    pos = pos_col + zero
    pos_row = to_row(pos_col)
    same = jnp.where(pos == pos_row + zero, 1, 0) * jnp.where(pos >= 0, 1, 0) * jnp.where(r < l, 1, 0)
    prev = jnp.max(jnp.where(same > 0, r, -1), axis=0, keepdims=True)
    last = jnp.max(jnp.where(pos == l, r, -1), axis=0, keepdims=True)
    own = jnp.where((r1 >> 4) == col, 1, 0)
    own_at = own * jnp.where(enc_col > 0, 1, 0)
    base = jnp.max(jnp.where((own_at * enc_col + zero) == l + 1, r & 15, -1), axis=0, keepdims=True)
    base = jnp.where(base < 0, BLANK, PRODUCTS + base)
    base_col = lanes(jnp.where(pos == l, base + zero, 0))
    base_of = to_row(jnp.where(pos_col < 0, BLANK, base_col))
    a_index = (((kk >> 3) ^ (x & 1)) << 3) | (kk & 7)
    tab_v[0:1, :] = to_row(a_index)
    tab_v[1:2, :] = jnp.where(prev < 0, base_of, prev)
    tab_v[2:3, :] = jnp.where(last < 0, base, last)
    tab_v[3:4, :] = to_row(good)
    tab_v[4:5, :] = to_row(((t_col >> 4) << 3) + (t_col & 7))
    tab_v[5:6, :] = to_row(src)
    tab_v[6:8, :] = jnp.zeros((2, 128), jnp.int32)


def kernel(
    cell_in, count_in, mcol_in, mlive_in, f_ref, a_ref, out_ref,
    cell_ref, count_ref, mcol_ref, mlive_ref,
    a0, a1, a2, a3, a4, a5, a6, a7, fl, fu, s_ref, picked, mb, mm, mb_in, mm_in, tab_v, tab, gains,
    a_send, a_recv, f_send, f_recv, m_send, m_recv, g_send, g_recv, local_sem,
):
    row, col = lax.axis_index("row"), lax.axis_index("col")
    y, x, z, core = row >> 2, row & 3, col >> 1, col & 1
    groups = (a0, a1, a2, a3, a4, a5, a6, a7)

    barrier = pltpu.get_barrier_semaphore()
    for d in NEAR_ROW:
        pl.semaphore_signal(barrier, inc=1, device_id=(row ^ d, col), device_id_type=MESH)
    for d in NEAR_COL:
        pl.semaphore_signal(barrier, inc=1, device_id=(row, col ^ d), device_id_type=MESH)

    scalars = [
        pltpu.make_async_copy(there, here, local_sem.at[5 + i])
        for i, (there, here) in enumerate(
            ((cell_in, cell_ref), (count_in, count_ref), (mcol_in, mcol_ref), (mlive_in, mlive_ref))
        )
    ]
    for copy in scalars:
        copy.start()
    local = [
        pltpu.make_async_copy(a_ref, a0.at[pl.ds(0, 8)], local_sem.at[0]),
        pltpu.make_async_copy(f_ref.at[pl.ds(0, 8)], fl.at[pl.ds(col * 8, 8)], local_sem.at[1]),
        pltpu.make_async_copy(f_ref.at[pl.ds(8, 8)], fu.at[pl.ds(col * 8, 8)], local_sem.at[2]),
    ]
    for copy in local:
        copy.start()

    pl.semaphore_wait(barrier, len(NEAR_ROW) + len(NEAR_COL))

    started = []

    def send(src, dst, send_sem, recv_sem, device, keep=True):
        copy = pltpu.make_async_remote_copy(
            src_ref=src, dst_ref=dst, send_sem=send_sem, recv_sem=recv_sem,
            device_id=device, device_id_type=MESH,
        )
        copy.start()
        if keep:
            started.append(copy)
        return copy

    def arrived(ref, sem):
        pltpu.make_async_remote_copy(
            src_ref=ref, dst_ref=ref, send_sem=m_send.at[0], recv_sem=sem,
            device_id=(row ^ 1, col), device_id_type=MESH,
        ).wait_recv()

    def a_block(dy, dx, q):
        return groups[dy * 2 + (dx >> 1)].at[pl.ds((dx & 1) * 8 + 2 * q, 2)]

    a_here, f_here = set(), set()

    def a_wait(dy, dx, *quarters):
        for q in quarters:
            if (dy, dx) != (0, 0) and (dy, dx, q) not in a_here:
                a_here.add((dy, dx, q))
                arrived(a_block(dy, dx, q), a_recv.at[(dy * 4 + dx) * 4 + q])

    def f_source(dz, dc):
        return ((z ^ dz) << 1) | (core ^ dc)

    def f_block(dz, dc, u, n=2):
        upper, first = u // 4, 2 * (u % 4)
        return (fu if upper else fl).at[pl.ds(f_source(dz, dc) * 8 + first, n)]

    def f_wait(dz, *units):
        for u in units:
            if dz and (dz, u) not in f_here:
                f_here.add((dz, u))
                arrived(f_block(dz, 0, u), f_recv.at[dz * 8 + u])

    def sib_wait(upper):
        for dz in range(4):
            for u in (4 * upper, 4 * upper + 2):
                arrived(f_block(dz, 1, u, 4), f_recv.at[32 + dz * 4 + u // 2])

    def sib_send(dz, *halves):
        for h in halves:
            f_wait(dz, 2 * h, 2 * h + 1)
            src = f_ref.at[pl.ds(4 * h, 4)] if dz == 0 else f_block(dz, 0, 2 * h, 4)
            send(
                src, f_block(dz, 0, 2 * h, 4), f_send.at[24 + dz * 4 + h],
                f_recv.at[32 + dz * 4 + h], (row, col ^ 1),
            )

    def x_link(near, part):
        turn = [((0, 0), 0), ((0, 0), 1), ((0, 0), 2), ((0, near), part), ((0, 0), 3)]
        turn += [((dy, 0), q) for dy in (1, 3, 2) for q in (2, 3)]
        return turn + [((dy, near), part + 2) for dy in (0, 1, 3, 2)]

    def y_link(near, part):
        turn = [((0, 0), 2), ((0, 0), 3), ((0, 0), 0), ((near, 0), part + 2), ((0, 0), 1)]
        turn += [((0, dx), q) for dx in (1, 3, 2) for q in (0, 1)]
        return turn + [((near, dx), part) for dx in (0, 1, 3, 2)]

    def z_link(near, part):
        turn = [(0, u) for u in range(4)] + [(near, 2 * part), (near, 2 * part + 1)]
        return turn + [(0, u) for u in range(4, 8)] + [(near, 4 + 2 * part), (near, 5 + 2 * part)]

    a_links = ((XA, x_link(3, 0)), (YA, y_link(3, 0)), (XB, x_link(1, 1)), (YB, y_link(1, 1)))
    z_links = ((1, z_link(3, 0)), (3, z_link(1, 1)))
    flying = {}

    def pace(link):
        queue = flying.setdefault(link, [])
        if len(queue) == DEPTH:
            queue.pop(0).wait_send()
        return queue

    def turn(k):
        for i, ((ly, lx), order) in enumerate(a_links):
            (dy, dx), q = order[k]
            queue = pace(i)
            a_wait(dy, dx, q)
            src = a_ref.at[pl.ds(2 * q, 2)] if (dy, dx) == (0, 0) else a_block(dy, dx, q)
            there = (dy ^ ly, dx ^ lx)
            queue.append(send(
                src, a_block(*there, q), a_send.at[i * 15 + k],
                a_recv.at[(there[0] * 4 + there[1]) * 4 + q],
                (((y ^ ly) << 2) | (x ^ lx), col), False,
            ))
        if k < 12:
            for i, (lz, order) in enumerate(z_links):
                dz, u = order[k]
                queue = pace(4 + i)
                f_wait(dz, u)
                src = f_ref.at[pl.ds(2 * u, 2)] if dz == 0 else f_block(dz, 0, u)
                queue.append(send(
                    src, f_block(dz, 0, u), f_send.at[i * 12 + k],
                    f_recv.at[(dz ^ lz) * 8 + u], (row, f_source(lz, 0)), False,
                ))

    def own_rows():
        for copy in scalars:
            copy.wait()
        lane = lax.broadcasted_iota(jnp.int32, (8, 128), 1)
        own_b, own_m = jnp.zeros((8, 128), jnp.int32), jnp.zeros((8, 128), jnp.int32)
        for s in range(16):
            value = jnp.where(s < count_ref[0, 0], cell_ref[0, s] + 1, 0)
            own_b = jnp.where(lane == col * 16 + s, value, own_b)
        for s in range(8):
            value = jnp.where(mlive_ref[0, s] > 0, mcol_ref[0, s] + 1, 0)
            own_m = jnp.where(lane == row * 8 + s, value, own_m)
        mb[0] = own_b
        mm[0] = own_m

    def m_exchange(k):
        if k < 4:
            send(mm.at[k], mm_in.at[k], m_send.at[k], m_recv.at[k], (row ^ NEAR_ROW[k], col))
        if k < 3:
            send(mb.at[k], mb_in.at[k], m_send.at[4 + k], m_recv.at[4 + k], (row, col ^ NEAR_COL[k]))

    def m_add(k):
        if k < 4:
            arrived(mm_in.at[k], m_recv.at[k])
            mm[k + 1] = mm[k] + mm_in[k]
        if k < 3:
            arrived(mb_in.at[k], m_recv.at[4 + k])
            mb[k + 1] = mb[k] + mb_in[k]

    s_ref[BLANK] = jnp.zeros((TILE, TILE), jnp.float32)

    def group_of(n):
        dy, q = ORDER[n]
        return groups[dy * 2 + q], ((y ^ dy) << 1) | ((x >> 1) ^ q)

    def add_product(o, f_tile, a_tile, gain):
        before = s_ref[tab[1, o]]
        after = jnp.dot(f_tile, a_tile, preferred_element_type=jnp.float32) + before
        s_ref[o] = after
        more = (jnp.minimum(1.0, after) - jnp.minimum(1.0, before)).reshape(8, TILE // 8, TILE)
        return gain + jnp.where(tab[3, o] > 0, jnp.sum(more, axis=0), 0.0)

    def products(n, gain):
        a_group, source = group_of(n)
        for dx in (0, 1):
            a_wait(ORDER[n][0], 2 * ORDER[n][1] + dx, 0, 1, 2, 3)

        def lower(s, gain):
            o = n * 8 + s
            return add_product(o, fl[source * 8 + s], a_group[tab[0, o]], gain)

        gain = lax.fori_loop(0, 8, lower, gain, unroll=UNROLL)

        def upper(j, carry):
            tile = a_group[tab[0, LOWER + j]]
            if n == 0:
                picked[j] = tile
            else:
                picked[j] = jnp.where(tab[5, LOWER + j] == source, tile, picked[j])
            return carry

        lax.fori_loop(0, 8, upper, 0)
        return gain

    total = jnp.zeros((TILE // 8, TILE), jnp.float32)
    for k in range(15):
        turn(k)
        if k == 0:
            own_rows()
            m_exchange(0)
        if k in (1, 3, 5):
            m_add(k // 2)
            m_exchange(k // 2 + 1)
        if k == 2:
            sib_send(0, 0, 1, 2, 3)
        if k == 6:
            sib_send(1, 0, 1)
            sib_send(3, 0, 1)
        if k == 7:
            m_add(3)
            tables(tab_v, mb[3, 0:1, :], mm[4, 0:1, :], y, x, col)
            to_scalars = pltpu.make_async_copy(tab_v, tab, local_sem.at[4])
            to_scalars.start()
            to_scalars.wait()
        if k == 8:
            sib_send(2, 0, 1)
        if k == 10:
            for copy in local:
                copy.wait()
            sib_wait(0)

            def widen(s, carry):
                s_ref[PRODUCTS + s] = fl[col * 8 + s].astype(jnp.float32)
                s_ref[PRODUCTS + 8 + s] = fu[col * 8 + s].astype(jnp.float32)
                return carry

            lax.fori_loop(0, 8, widen, 0)
            total = products(0, total)
        if k == 11:
            total = products(1, total)
            total = products(2, total)
        if k == 12:
            sib_send(1, 2, 3)
            sib_send(3, 2, 3)
        if k == 13:
            total = products(3, total)
    sib_send(2, 2, 3)
    for n in range(4, 8):
        total = products(n, total)
    sib_wait(1)

    def spilled(j, gain):
        o = LOWER + j
        return add_product(o, fu[tab[4, o]], picked[j], gain)

    total = lax.fori_loop(0, 8, spilled, total, unroll=UNROLL)

    def output(c, carry):
        for i in range(2):
            out_ref[pl.ds(i * TILE, TILE), pl.ds(pl.multiple_of(c * TILE, TILE), TILE)] = jnp.minimum(
                1.0, s_ref[tab[2, i * 16 + c]]
            ).astype(jnp.bfloat16)
        return carry

    total = jnp.sum(total.reshape(TILE // 64, 8, TILE), axis=0)
    part = total[:, :128] + total[:, 128:]
    for k, n in enumerate((N_ROW, N_COL)):
        gains[k, 0] = part
        for d in FAR_FIRST if k == 0 else range(n - 1, 0, -1):
            device = (row, col ^ d) if k else (row ^ d, col)
            send(gains.at[k, 0], gains.at[k, d], g_send.at[k * N_ROW + d], g_recv.at[k], device)
        if k == 0:
            lax.fori_loop(0, 16, output, 0)
        arrived(gains.at[k, pl.ds(1, n - 1)], g_recv.at[k])
        parts = [gains[k, d] for d in range(n)]
        while len(parts) > 1:
            parts = [parts[2 * i] + parts[2 * i + 1] for i in range(len(parts) // 2)]
        part = parts[0]
    rest = jnp.zeros((16, 128), jnp.float32) + jnp.sum(part) * (1.0 / 268435456.0)
    for k in range(3):
        piece = rest.astype(jnp.bfloat16)
        out_ref[pl.ds(2 * TILE, 16), pl.ds(k * 128, 128)] = piece
        rest = rest - piece.astype(jnp.float32)
    for queue in flying.values():
        started.extend(queue)
    for copy in started:
        copy.wait_send()


def store_kernel(from_ref, to_ref, gain_ref, gain_s, sem):
    rows = [pl.ds(128 * i, 128) for i in range(4)]
    copies = [pltpu.make_async_copy(from_ref.at[r], to_ref.at[r], sem.at[i]) for i, r in enumerate(rows)]
    for copy in copies:
        copy.start()
    gain = jnp.zeros((16, 128), jnp.float32)
    for k in (2, 1, 0):
        gain += from_ref[pl.ds(2 * TILE, 16), pl.ds(k * 128, 128)].astype(jnp.float32)
    gain_s[0, 0] = gain[0, 0]
    copies.append(pltpu.make_async_copy(gain_s, gain_ref, sem.at[4]))
    copies[-1].start()
    for copy in copies:
        copy.wait()


def on_device(band_tiles, band_cell, band_count, matrix_tiles, matrix_col, matrix_live):
    vmem = pl.BlockSpec(memory_space=pltpu.VMEM)
    hbm = pl.BlockSpec(memory_space=pl.ANY)
    tiles = (TILE, TILE)
    both = pl.pallas_call(
        kernel,
        out_shape=pltpu.VMEM((2 * TILE + 16, 16 * TILE), jnp.bfloat16),
        in_specs=[hbm] * 6,
        out_specs=vmem,
        scratch_shapes=[pltpu.SMEM((1, n), jnp.int32) for n in (16, 1, 8, 8)]
        + [pltpu.VMEM((16, *tiles), jnp.bfloat16)] * 8
        + [
            pltpu.VMEM((LOWER, *tiles), jnp.bfloat16),
            pltpu.VMEM((LOWER, *tiles), jnp.bfloat16),
            pltpu.VMEM((BLANK + 1, *tiles), jnp.float32),
            pltpu.VMEM((8, *tiles), jnp.bfloat16),
            pltpu.VMEM((4, 8, 128), jnp.int32),
            pltpu.VMEM((5, 8, 128), jnp.int32),
            pltpu.VMEM((3, 8, 128), jnp.int32),
            pltpu.VMEM((4, 8, 128), jnp.int32),
            pltpu.VMEM((8, 128), jnp.int32),
            pltpu.SMEM((8, 128), jnp.int32),
            pltpu.VMEM((2, N_ROW, 8, 128), jnp.float32),
            pltpu.SemaphoreType.DMA((60,)),
            pltpu.SemaphoreType.DMA((64,)),
            pltpu.SemaphoreType.DMA((40,)),
            pltpu.SemaphoreType.DMA((48,)),
            pltpu.SemaphoreType.DMA((7,)),
            pltpu.SemaphoreType.DMA((7,)),
            pltpu.SemaphoreType.DMA((24,)),
            pltpu.SemaphoreType.DMA((2,)),
            pltpu.SemaphoreType.DMA((9,)),
        ],
        compiler_params=pltpu.CompilerParams(
            collective_id=0, has_side_effects=True, vmem_limit_bytes=57 * 1024 * 1024
        ),
    )(band_cell, band_count, matrix_col, matrix_live, band_tiles[0], matrix_tiles[0])
    reached, gain = pl.pallas_call(
        store_kernel,
        out_shape=(
            jax.ShapeDtypeStruct((2 * TILE, 16 * TILE), jnp.bfloat16),
            jax.ShapeDtypeStruct((1, 1), jnp.float32),
        ),
        in_specs=[vmem],
        out_specs=(hbm, hbm),
        scratch_shapes=[pltpu.SMEM((1, 1), jnp.float32), pltpu.SemaphoreType.DMA((5,))],
        compiler_params=pltpu.CompilerParams(vmem_limit_bytes=1024 * 1024),
    )(pltpu.with_memory_space_constraint(both, pltpu.VMEM))
    return reached, gain.reshape(())


def solution(mesh):
    placed = P("row", "col")
    tiled = P("row", "col", None, None)
    return jax.shard_map(
        on_device, mesh=mesh,
        in_specs=(tiled, placed, placed, tiled, placed, placed),
        out_specs=(placed, P()), check_vma=False,
    )
```

```python
import functools

import jax
import jax.numpy as jnp
from jax import lax
from jax.experimental import pallas as pl
from jax.experimental.pallas import tpu as pltpu
from jax.sharding import PartitionSpec as P

TILE = 256
N_ROW, N_COL = 16, 8
SPOTS = 32
LOWER = 64
PRODUCTS = 72
BLANK = PRODUCTS + 16
ORDER = ((0, 0), (1, 0), (3, 0), (0, 1), (1, 1), (2, 0), (3, 1), (2, 1))
UNROLL = 8
DEPTH = 2
XA, XB, YA, YB = (0, 1), (0, 3), (1, 0), (3, 0)
NEAR_ROW, NEAR_COL = (1, 3, 4, 12), (2, 6, 1)
CHIPS = 64
MESH = pl.DeviceIdType.MESH


def tables(tab_v, enc_row, menc_row, y, x, col):
    shape = (128, 128)
    r = lax.broadcasted_iota(jnp.int32, shape, 0)
    l = lax.broadcasted_iota(jnp.int32, shape, 1)
    r1 = lax.broadcasted_iota(jnp.int32, (128, 1), 0)
    zero = jnp.zeros(shape, jnp.int32)
    eye = r == l

    def lanes(v):
        return jnp.sum(v, axis=1, keepdims=True)

    def to_row(column):
        return jnp.sum(jnp.where(eye, column + zero, 0), axis=0, keepdims=True)

    enc = enc_row + zero
    enc_col = lanes(jnp.where(eye, enc, 0))
    up_col = jnp.where(enc_col > 0, 1, 0) * ((r1 >> 3) & 1)
    rank_row = jnp.sum(jnp.where(r < l, up_col + zero, 0), axis=0, keepdims=True)
    up = jnp.where(enc > 0, 1, 0) * ((l >> 3) & 1)
    group = r1 >> 3
    source = jnp.zeros((128, 1), jnp.int32)
    for n, (dy, q) in enumerate(ORDER):
        source = jnp.where(group == n, ((y ^ dy) << 1) | ((x >> 1) ^ q), source)
    slot = (source << 4) + (r1 & 7)
    low_hit = jnp.where(l == slot + zero, 1, 0)
    up_hit = up * jnp.where(rank_row + zero == r - LOWER, 1, 0)
    pick = jnp.where(r < LOWER, low_hit, up_hit)
    cell_col = lanes(pick * enc)
    t_col = lanes(pick * l)
    cell = jnp.maximum(cell_col - 1, 0)
    kk, src = cell & 15, t_col >> 4
    menc_col = lanes(jnp.where(l == ((src << 4) + kk) + zero, menc_row + zero, 0))
    good = jnp.where(cell_col > 0, 1, 0) * jnp.where(menc_col > 0, 1, 0)
    pos_col = jnp.where(good > 0, ((cell >> 4) << 4) + menc_col - 1, -1)
    pos = pos_col + zero
    pos_row = to_row(pos_col)
    same = jnp.where(pos == pos_row + zero, 1, 0) * jnp.where(pos >= 0, 1, 0) * jnp.where(r < l, 1, 0)
    prev = jnp.max(jnp.where(same > 0, r, -1), axis=0, keepdims=True)
    last = jnp.max(jnp.where(pos == l, r, -1), axis=0, keepdims=True)
    own = jnp.where((r1 >> 4) == col, 1, 0)
    own_at = own * jnp.where(enc_col > 0, 1, 0)
    base = jnp.max(jnp.where((own_at * enc_col + zero) == l + 1, r & 15, -1), axis=0, keepdims=True)
    base = jnp.where(base < 0, BLANK, PRODUCTS + base)
    base_col = lanes(jnp.where(pos == l, base + zero, 0))
    base_of = to_row(jnp.where(pos_col < 0, BLANK, base_col))
    a_index = (((kk >> 3) ^ (x & 1)) << 3) | (kk & 7)
    tab_v[0:1, :] = to_row(a_index)
    tab_v[1:2, :] = jnp.where(prev < 0, base_of, prev)
    tab_v[2:3, :] = jnp.where(last < 0, base, last)
    tab_v[3:4, :] = to_row(good)
    tab_v[4:5, :] = to_row(((t_col >> 4) << 3) + (t_col & 7))
    tab_v[5:6, :] = to_row(src)
    tab_v[6:8, :] = jnp.zeros((2, 128), jnp.int32)


def kernel(
    cell_in, count_in, mcol_in, mlive_in, f_ref, a_ref, out_ref,
    cell_ref, count_ref, mcol_ref, mlive_ref,
    a0, a1, a2, a3, a4, a5, a6, a7, fl, fu, s_ref, picked, mb, mm, mb_in, mm_in, tab_v, tab, pair, gains,
    a_send, a_recv, f_send, f_recv, m_send, m_recv, g_send, g_recv, plane_sem, local_sem,
):
    row, col = lax.axis_index("row"), lax.axis_index("col")
    y, x, z, core = row >> 2, row & 3, col >> 1, col & 1
    groups = (a0, a1, a2, a3, a4, a5, a6, a7)

    barrier = pltpu.get_barrier_semaphore()
    for d in NEAR_ROW:
        pl.semaphore_signal(barrier, inc=1, device_id=(row ^ d, col), device_id_type=MESH)
    for d in NEAR_COL:
        pl.semaphore_signal(barrier, inc=1, device_id=(row, col ^ d), device_id_type=MESH)

    scalars = [
        pltpu.make_async_copy(there, here, local_sem.at[5 + i])
        for i, (there, here) in enumerate(
            ((cell_in, cell_ref), (count_in, count_ref), (mcol_in, mcol_ref), (mlive_in, mlive_ref))
        )
    ]
    for copy in scalars:
        copy.start()
    local = [
        pltpu.make_async_copy(a_ref, a0.at[pl.ds(0, 8)], local_sem.at[0]),
        pltpu.make_async_copy(f_ref.at[pl.ds(0, 8)], fl.at[pl.ds(col * 8, 8)], local_sem.at[1]),
        pltpu.make_async_copy(f_ref.at[pl.ds(8, 8)], fu.at[pl.ds(col * 8, 8)], local_sem.at[2]),
    ]
    for copy in local:
        copy.start()

    pl.semaphore_wait(barrier, len(NEAR_ROW) + len(NEAR_COL))

    started = []

    def send(src, dst, send_sem, recv_sem, device, keep=True):
        copy = pltpu.make_async_remote_copy(
            src_ref=src, dst_ref=dst, send_sem=send_sem, recv_sem=recv_sem,
            device_id=device, device_id_type=MESH,
        )
        copy.start()
        if keep:
            started.append(copy)
        return copy

    def arrived(ref, sem):
        pltpu.make_async_remote_copy(
            src_ref=ref, dst_ref=ref, send_sem=m_send.at[0], recv_sem=sem,
            device_id=(row ^ 1, col), device_id_type=MESH,
        ).wait_recv()

    def a_block(dy, dx, q):
        return groups[dy * 2 + (dx >> 1)].at[pl.ds((dx & 1) * 8 + 2 * q, 2)]

    a_here, f_here = set(), set()

    def a_wait(dy, dx, *quarters):
        for q in quarters:
            if (dy, dx) != (0, 0) and (dy, dx, q) not in a_here:
                a_here.add((dy, dx, q))
                arrived(a_block(dy, dx, q), a_recv.at[(dy * 4 + dx) * 4 + q])

    def f_source(dz, dc):
        return ((z ^ dz) << 1) | (core ^ dc)

    def f_block(dz, dc, u, n=2):
        upper, first = u // 4, 2 * (u % 4)
        return (fu if upper else fl).at[pl.ds(f_source(dz, dc) * 8 + first, n)]

    def f_wait(dz, *units):
        for u in units:
            if dz and (dz, u) not in f_here:
                f_here.add((dz, u))
                arrived(f_block(dz, 0, u), f_recv.at[dz * 8 + u])

    def sib_wait(upper):
        for dz in range(4):
            for u in (4 * upper, 4 * upper + 2):
                arrived(f_block(dz, 1, u, 4), f_recv.at[32 + dz * 4 + u // 2])

    def sib_send(dz, *halves):
        for h in halves:
            f_wait(dz, 2 * h, 2 * h + 1)
            src = f_ref.at[pl.ds(4 * h, 4)] if dz == 0 else f_block(dz, 0, 2 * h, 4)
            send(
                src, f_block(dz, 0, 2 * h, 4), f_send.at[24 + dz * 4 + h],
                f_recv.at[32 + dz * 4 + h], (row, col ^ 1),
            )

    def x_link(near, part):
        turn = [((0, 0), 0), ((0, 0), 1), ((0, 0), 2), ((0, near), part), ((0, 0), 3)]
        turn += [((dy, 0), q) for dy in (1, 3, 2) for q in (2, 3)]
        return turn + [((dy, near), part + 2) for dy in (0, 1, 3, 2)]

    def y_link(near, part):
        turn = [((0, 0), 2), ((0, 0), 3), ((0, 0), 0), ((near, 0), part + 2), ((0, 0), 1)]
        turn += [((0, dx), q) for dx in (1, 3, 2) for q in (0, 1)]
        return turn + [((near, dx), part) for dx in (0, 1, 3, 2)]

    def z_link(near, part):
        turn = [(0, u) for u in range(4)] + [(near, 2 * part), (near, 2 * part + 1)]
        return turn + [(0, u) for u in range(4, 8)] + [(near, 4 + 2 * part), (near, 5 + 2 * part)]

    a_links = ((XA, x_link(3, 0)), (YA, y_link(3, 0)), (XB, x_link(1, 1)), (YB, y_link(1, 1)))
    z_links = ((1, z_link(3, 0)), (3, z_link(1, 1)))
    flying = {}

    def pace(link):
        queue = flying.setdefault(link, [])
        if len(queue) == DEPTH:
            queue.pop(0).wait_send()
        return queue

    def turn(k):
        for i, ((ly, lx), order) in enumerate(a_links):
            (dy, dx), q = order[k]
            queue = pace(i)
            a_wait(dy, dx, q)
            src = a_ref.at[pl.ds(2 * q, 2)] if (dy, dx) == (0, 0) else a_block(dy, dx, q)
            there = (dy ^ ly, dx ^ lx)
            queue.append(send(
                src, a_block(*there, q), a_send.at[i * 15 + k],
                a_recv.at[(there[0] * 4 + there[1]) * 4 + q],
                (((y ^ ly) << 2) | (x ^ lx), col), False,
            ))
        if k < 12:
            for i, (lz, order) in enumerate(z_links):
                dz, u = order[k]
                queue = pace(4 + i)
                f_wait(dz, u)
                src = f_ref.at[pl.ds(2 * u, 2)] if dz == 0 else f_block(dz, 0, u)
                queue.append(send(
                    src, f_block(dz, 0, u), f_send.at[i * 12 + k],
                    f_recv.at[(dz ^ lz) * 8 + u], (row, f_source(lz, 0)), False,
                ))

    def own_rows():
        for copy in scalars:
            copy.wait()
        lane = lax.broadcasted_iota(jnp.int32, (8, 128), 1)
        own_b, own_m = jnp.zeros((8, 128), jnp.int32), jnp.zeros((8, 128), jnp.int32)
        for s in range(16):
            value = jnp.where(s < count_ref[0, 0], cell_ref[0, s] + 1, 0)
            own_b = jnp.where(lane == col * 16 + s, value, own_b)
        for s in range(8):
            value = jnp.where(mlive_ref[0, s] > 0, mcol_ref[0, s] + 1, 0)
            own_m = jnp.where(lane == row * 8 + s, value, own_m)
        mb[0] = own_b
        mm[0] = own_m

    def m_exchange(k):
        if k < 4:
            send(mm.at[k], mm_in.at[k], m_send.at[k], m_recv.at[k], (row ^ NEAR_ROW[k], col))
        if k < 3:
            send(mb.at[k], mb_in.at[k], m_send.at[4 + k], m_recv.at[4 + k], (row, col ^ NEAR_COL[k]))

    def m_add(k):
        if k < 4:
            arrived(mm_in.at[k], m_recv.at[k])
            mm[k + 1] = mm[k] + mm_in[k]
        if k < 3:
            arrived(mb_in.at[k], m_recv.at[4 + k])
            mb[k + 1] = mb[k] + mb_in[k]

    s_ref[BLANK] = jnp.zeros((TILE, TILE), jnp.float32)

    def group_of(n):
        dy, q = ORDER[n]
        return groups[dy * 2 + q], ((y ^ dy) << 1) | ((x >> 1) ^ q)

    def add_product(o, f_tile, a_tile, gain):
        before = s_ref[tab[1, o]]
        after = jnp.dot(f_tile, a_tile, preferred_element_type=jnp.float32) + before
        s_ref[o] = after
        more = (jnp.minimum(1.0, after) - jnp.minimum(1.0, before)).reshape(8, TILE // 8, TILE)
        return gain + jnp.where(tab[3, o] > 0, jnp.sum(more, axis=0), 0.0)

    def products(n, gain):
        a_group, source = group_of(n)
        for dx in (0, 1):
            a_wait(ORDER[n][0], 2 * ORDER[n][1] + dx, 0, 1, 2, 3)

        def lower(s, gain):
            o = n * 8 + s
            return add_product(o, fl[source * 8 + s], a_group[tab[0, o]], gain)

        gain = lax.fori_loop(0, 8, lower, gain, unroll=UNROLL)

        def upper(j, carry):
            tile = a_group[tab[0, LOWER + j]]
            if n == 0:
                picked[j] = tile
            else:
                picked[j] = jnp.where(tab[5, LOWER + j] == source, tile, picked[j])
            return carry

        lax.fori_loop(0, 8, upper, 0)
        return gain

    total = jnp.zeros((TILE // 8, TILE), jnp.float32)
    for k in range(15):
        turn(k)
        if k == 0:
            own_rows()
            m_exchange(0)
        if k in (1, 3, 5):
            m_add(k // 2)
            m_exchange(k // 2 + 1)
        if k == 2:
            sib_send(0, 0, 1, 2, 3)
        if k == 6:
            sib_send(1, 0, 1)
            sib_send(3, 0, 1)
        if k == 7:
            m_add(3)
            tables(tab_v, mb[3, 0:1, :], mm[4, 0:1, :], y, x, col)
            to_scalars = pltpu.make_async_copy(tab_v, tab, local_sem.at[4])
            to_scalars.start()
            to_scalars.wait()
        if k == 8:
            sib_send(2, 0, 1)
            for e in (1, 2, 3):
                pl.semaphore_signal(plane_sem, inc=1, device_id=(row, col ^ (2 * e)), device_id_type=MESH)
        if k == 10:
            for copy in local:
                copy.wait()
            sib_wait(0)

            def widen(s, carry):
                s_ref[PRODUCTS + s] = fl[col * 8 + s].astype(jnp.float32)
                s_ref[PRODUCTS + 8 + s] = fu[col * 8 + s].astype(jnp.float32)
                return carry

            lax.fori_loop(0, 8, widen, 0)
            total = products(0, total)
        if k == 11:
            total = products(1, total)
            total = products(2, total)
        if k == 12:
            pl.semaphore_wait(plane_sem, 3)
            sib_send(1, 2, 3)
            sib_send(3, 2, 3)
        if k == 13:
            total = products(3, total)
    sib_send(2, 2, 3)
    for n in range(4, 8):
        total = products(n, total)
    sib_wait(1)

    def spilled(j, gain):
        o = LOWER + j
        return add_product(o, fu[tab[4, o]], picked[j], gain)

    total = lax.fori_loop(0, 8, spilled, total, unroll=UNROLL)

    def output(c, carry):
        for i in range(2):
            out_ref[pl.ds(i * TILE, TILE), pl.ds(pl.multiple_of(c * TILE, TILE), TILE)] = jnp.minimum(
                1.0, s_ref[tab[2, i * 16 + c]]
            ).astype(jnp.bfloat16)
        return carry

    total = jnp.sum(total.reshape(TILE // 64, 8, TILE), axis=0)
    pair[0] = total[:, :128] + total[:, 128:]
    send(pair.at[0], pair.at[1], g_send.at[0], g_recv.at[0], (row, col ^ 1))
    lax.fori_loop(0, 6, output, 0)
    arrived(pair.at[1], g_recv.at[0])
    gains[0] = pair[0] + pair[1]
    me = (z << 4) | row

    def to_chip(n, carry):
        @pl.when(n != me)
        def _():
            to_row, to_z = n & 15, n >> 4
            pltpu.make_async_remote_copy(
                src_ref=gains.at[0], dst_ref=gains.at[((row ^ to_row) << 2) | (z ^ to_z)],
                send_sem=g_send.at[1], recv_sem=g_recv.at[1],
                device_id=(to_row, (to_z << 1) | core), device_id_type=MESH,
            ).start()

        return carry

    lax.fori_loop(0, CHIPS, to_chip, 0, unroll=4)
    lax.fori_loop(6, 16, output, 0)
    others = gains.at[pl.ds(1, CHIPS - 1)]
    arrived(others, g_recv.at[1])
    part = gains[...]
    while part.shape[0] > 1:
        part = part.reshape(part.shape[0] // 2, 2, 8, 128)
        part = part[:, 0] + part[:, 1]
    rest = jnp.zeros((16, 128), jnp.float32) + jnp.sum(part) * (1.0 / 268435456.0)
    for k in range(3):
        piece = rest.astype(jnp.bfloat16)
        out_ref[pl.ds(2 * TILE, 16), pl.ds(k * 128, 128)] = piece
        rest = rest - piece.astype(jnp.float32)
    for queue in flying.values():
        started.extend(queue)
    for copy in started:
        copy.wait_send()
    pltpu.make_async_remote_copy(
        src_ref=others, dst_ref=others, send_sem=g_send.at[1], recv_sem=g_recv.at[1],
        device_id=(row ^ 1, col), device_id_type=MESH,
    ).wait_send()


def store_kernel(from_ref, to_ref, gain_ref, gain_s, sem):
    rows = [pl.ds(128 * i, 128) for i in range(4)]
    copies = [pltpu.make_async_copy(from_ref.at[r], to_ref.at[r], sem.at[i]) for i, r in enumerate(rows)]
    for copy in copies:
        copy.start()
    gain = jnp.zeros((16, 128), jnp.float32)
    for k in (2, 1, 0):
        gain += from_ref[pl.ds(2 * TILE, 16), pl.ds(k * 128, 128)].astype(jnp.float32)
    gain_s[0, 0] = gain[0, 0]
    copies.append(pltpu.make_async_copy(gain_s, gain_ref, sem.at[4]))
    copies[-1].start()
    for copy in copies:
        copy.wait()


def on_device(band_tiles, band_cell, band_count, matrix_tiles, matrix_col, matrix_live):
    vmem = pl.BlockSpec(memory_space=pltpu.VMEM)
    hbm = pl.BlockSpec(memory_space=pl.ANY)
    tiles = (TILE, TILE)
    both = pl.pallas_call(
        kernel,
        out_shape=pltpu.VMEM((2 * TILE + 16, 16 * TILE), jnp.bfloat16),
        in_specs=[hbm] * 6,
        out_specs=vmem,
        scratch_shapes=[pltpu.SMEM((1, n), jnp.int32) for n in (16, 1, 8, 8)]
        + [pltpu.VMEM((16, *tiles), jnp.bfloat16)] * 8
        + [
            pltpu.VMEM((LOWER, *tiles), jnp.bfloat16),
            pltpu.VMEM((LOWER, *tiles), jnp.bfloat16),
            pltpu.VMEM((BLANK + 1, *tiles), jnp.float32),
            pltpu.VMEM((8, *tiles), jnp.bfloat16),
            pltpu.VMEM((4, 8, 128), jnp.int32),
            pltpu.VMEM((5, 8, 128), jnp.int32),
            pltpu.VMEM((3, 8, 128), jnp.int32),
            pltpu.VMEM((4, 8, 128), jnp.int32),
            pltpu.VMEM((8, 128), jnp.int32),
            pltpu.SMEM((8, 128), jnp.int32),
            pltpu.VMEM((2, 8, 128), jnp.float32),
            pltpu.VMEM((64, 8, 128), jnp.float32),
            pltpu.SemaphoreType.DMA((60,)),
            pltpu.SemaphoreType.DMA((64,)),
            pltpu.SemaphoreType.DMA((40,)),
            pltpu.SemaphoreType.DMA((48,)),
            pltpu.SemaphoreType.DMA((7,)),
            pltpu.SemaphoreType.DMA((7,)),
            pltpu.SemaphoreType.DMA((2,)),
            pltpu.SemaphoreType.DMA((2,)),
            pltpu.SemaphoreType.REGULAR,
            pltpu.SemaphoreType.DMA((9,)),
        ],
        compiler_params=pltpu.CompilerParams(
            collective_id=0, has_side_effects=True, vmem_limit_bytes=57 * 1024 * 1024
        ),
    )(band_cell, band_count, matrix_col, matrix_live, band_tiles[0], matrix_tiles[0])
    reached, gain = pl.pallas_call(
        store_kernel,
        out_shape=(
            jax.ShapeDtypeStruct((2 * TILE, 16 * TILE), jnp.bfloat16),
            jax.ShapeDtypeStruct((1, 1), jnp.float32),
        ),
        in_specs=[vmem],
        out_specs=(hbm, hbm),
        scratch_shapes=[pltpu.SMEM((1, 1), jnp.float32), pltpu.SemaphoreType.DMA((5,))],
        compiler_params=pltpu.CompilerParams(vmem_limit_bytes=1024 * 1024),
    )(pltpu.with_memory_space_constraint(both, pltpu.VMEM))
    return reached, gain.reshape(())


def solution(mesh):
    placed = P("row", "col")
    tiled = P("row", "col", None, None)
    return jax.shard_map(
        on_device, mesh=mesh,
        in_specs=(tiled, placed, placed, tiled, placed, placed),
        out_specs=(placed, P()), check_vma=False,
    )
```

```python
import functools

import jax
import jax.numpy as jnp
from jax import lax
from jax.experimental import pallas as pl
from jax.experimental.pallas import tpu as pltpu
from jax.sharding import PartitionSpec as P

TILE = 256
N_ROW, N_COL = 16, 8
SPOTS = 32
LOWER = 64
PRODUCTS = 72
BLANK = PRODUCTS + 16
ORDER = ((0, 0), (1, 0), (3, 0), (0, 1), (1, 1), (2, 0), (3, 1), (2, 1))
UNROLL = 8
DEPTH = 2
XA, XB, YA, YB = (0, 1), (0, 3), (1, 0), (3, 0)
NEAR_ROW, NEAR_COL = (1, 3, 4, 12), (2, 6, 1)
CHIPS = 64
MESH = pl.DeviceIdType.MESH


def tables(tab_v, enc_row, menc_row, y, x, col):
    shape = (128, 128)
    r = lax.broadcasted_iota(jnp.int32, shape, 0)
    l = lax.broadcasted_iota(jnp.int32, shape, 1)
    r1 = lax.broadcasted_iota(jnp.int32, (128, 1), 0)
    zero = jnp.zeros(shape, jnp.int32)
    eye = r == l

    def lanes(v):
        return jnp.sum(v, axis=1, keepdims=True)

    def to_row(column):
        return jnp.sum(jnp.where(eye, column + zero, 0), axis=0, keepdims=True)

    enc = enc_row + zero
    enc_col = lanes(jnp.where(eye, enc, 0))
    up_col = jnp.where(enc_col > 0, 1, 0) * ((r1 >> 3) & 1)
    rank_row = jnp.sum(jnp.where(r < l, up_col + zero, 0), axis=0, keepdims=True)
    up = jnp.where(enc > 0, 1, 0) * ((l >> 3) & 1)
    group = r1 >> 3
    source = jnp.zeros((128, 1), jnp.int32)
    for n, (dy, q) in enumerate(ORDER):
        source = jnp.where(group == n, ((y ^ dy) << 1) | ((x >> 1) ^ q), source)
    slot = (source << 4) + (r1 & 7)
    low_hit = jnp.where(l == slot + zero, 1, 0)
    up_hit = up * jnp.where(rank_row + zero == r - LOWER, 1, 0)
    pick = jnp.where(r < LOWER, low_hit, up_hit)
    cell_col = lanes(pick * enc)
    t_col = lanes(pick * l)
    cell = jnp.maximum(cell_col - 1, 0)
    kk, src = cell & 15, t_col >> 4
    menc_col = lanes(jnp.where(l == ((src << 4) + kk) + zero, menc_row + zero, 0))
    good = jnp.where(cell_col > 0, 1, 0) * jnp.where(menc_col > 0, 1, 0)
    pos_col = jnp.where(good > 0, ((cell >> 4) << 4) + menc_col - 1, -1)
    pos = pos_col + zero
    pos_row = to_row(pos_col)
    same = jnp.where(pos == pos_row + zero, 1, 0) * jnp.where(pos >= 0, 1, 0) * jnp.where(r < l, 1, 0)
    prev = jnp.max(jnp.where(same > 0, r, -1), axis=0, keepdims=True)
    last = jnp.max(jnp.where(pos == l, r, -1), axis=0, keepdims=True)
    own = jnp.where((r1 >> 4) == col, 1, 0)
    own_at = own * jnp.where(enc_col > 0, 1, 0)
    base = jnp.max(jnp.where((own_at * enc_col + zero) == l + 1, r & 15, -1), axis=0, keepdims=True)
    base = jnp.where(base < 0, BLANK, PRODUCTS + base)
    base_col = lanes(jnp.where(pos == l, base + zero, 0))
    base_of = to_row(jnp.where(pos_col < 0, BLANK, base_col))
    a_index = (((kk >> 3) ^ (x & 1)) << 3) | (kk & 7)
    tab_v[0:1, :] = to_row(a_index)
    tab_v[1:2, :] = jnp.where(prev < 0, base_of, prev)
    tab_v[2:3, :] = jnp.where(last < 0, base, last)
    tab_v[3:4, :] = to_row(good)
    tab_v[4:5, :] = to_row(((t_col >> 4) << 3) + (t_col & 7))
    tab_v[5:6, :] = to_row(src)
    tab_v[6:8, :] = jnp.zeros((2, 128), jnp.int32)


def kernel(
    cell_in, count_in, mcol_in, mlive_in, f_ref, a_ref, out_ref,
    cell_ref, count_ref, mcol_ref, mlive_ref,
    a0, a1, a2, a3, a4, a5, a6, a7, fl, fu, s_ref, picked, mb, mm, mb_in, mm_in, tab_v, tab, pair, gains,
    a_send, a_recv, f_send, f_recv, m_send, m_recv, g_send, g_recv, plane_sem, local_sem,
):
    row, col = lax.axis_index("row"), lax.axis_index("col")
    y, x, z, core = row >> 2, row & 3, col >> 1, col & 1
    groups = (a0, a1, a2, a3, a4, a5, a6, a7)

    barrier = pltpu.get_barrier_semaphore()
    for d in NEAR_ROW:
        pl.semaphore_signal(barrier, inc=1, device_id=(row ^ d, col), device_id_type=MESH)
    for d in NEAR_COL:
        pl.semaphore_signal(barrier, inc=1, device_id=(row, col ^ d), device_id_type=MESH)

    scalars = [
        pltpu.make_async_copy(there, here, local_sem.at[5 + i])
        for i, (there, here) in enumerate(
            ((cell_in, cell_ref), (count_in, count_ref), (mcol_in, mcol_ref), (mlive_in, mlive_ref))
        )
    ]
    for copy in scalars:
        copy.start()
    local = [
        pltpu.make_async_copy(a_ref, a0.at[pl.ds(0, 8)], local_sem.at[0]),
        pltpu.make_async_copy(f_ref.at[pl.ds(0, 8)], fl.at[pl.ds(col * 8, 8)], local_sem.at[1]),
        pltpu.make_async_copy(f_ref.at[pl.ds(8, 8)], fu.at[pl.ds(col * 8, 8)], local_sem.at[2]),
    ]
    for copy in local:
        copy.start()

    pl.semaphore_wait(barrier, len(NEAR_ROW) + len(NEAR_COL))

    started = []

    def send(src, dst, send_sem, recv_sem, device, keep=True):
        copy = pltpu.make_async_remote_copy(
            src_ref=src, dst_ref=dst, send_sem=send_sem, recv_sem=recv_sem,
            device_id=device, device_id_type=MESH,
        )
        copy.start()
        if keep:
            started.append(copy)
        return copy

    def arrived(ref, sem):
        pltpu.make_async_remote_copy(
            src_ref=ref, dst_ref=ref, send_sem=m_send.at[0], recv_sem=sem,
            device_id=(row ^ 1, col), device_id_type=MESH,
        ).wait_recv()

    def a_block(dy, dx, q):
        return groups[dy * 2 + (dx >> 1)].at[pl.ds((dx & 1) * 8 + 2 * q, 2)]

    a_here, f_here = set(), set()

    def a_wait(dy, dx, *quarters):
        for q in quarters:
            if (dy, dx) != (0, 0) and (dy, dx, q) not in a_here:
                a_here.add((dy, dx, q))
                arrived(a_block(dy, dx, q), a_recv.at[(dy * 4 + dx) * 4 + q])

    def f_source(dz, dc):
        return ((z ^ dz) << 1) | (core ^ dc)

    def f_block(dz, dc, u, n=2):
        upper, first = u // 4, 2 * (u % 4)
        return (fu if upper else fl).at[pl.ds(f_source(dz, dc) * 8 + first, n)]

    def f_wait(dz, *units):
        for u in units:
            if dz and (dz, u) not in f_here:
                f_here.add((dz, u))
                arrived(f_block(dz, 0, u), f_recv.at[dz * 8 + u])

    def sib_wait(upper):
        for dz in range(4):
            for u in (4 * upper, 4 * upper + 2):
                arrived(f_block(dz, 1, u, 4), f_recv.at[32 + dz * 4 + u // 2])

    def sib_send(dz, *halves):
        for h in halves:
            f_wait(dz, 2 * h, 2 * h + 1)
            src = f_ref.at[pl.ds(4 * h, 4)] if dz == 0 else f_block(dz, 0, 2 * h, 4)
            send(
                src, f_block(dz, 0, 2 * h, 4), f_send.at[24 + dz * 4 + h],
                f_recv.at[32 + dz * 4 + h], (row, col ^ 1),
            )

    def x_link(near, part):
        turn = [((0, 0), 0), ((0, 0), 1), ((0, 0), 2), ((0, near), part), ((0, 0), 3)]
        turn += [((dy, 0), q) for dy in (1, 3, 2) for q in (2, 3)]
        return turn + [((dy, near), part + 2) for dy in (0, 1, 3, 2)]

    def y_link(near, part):
        turn = [((0, 0), 2), ((0, 0), 3), ((0, 0), 0), ((near, 0), part + 2), ((0, 0), 1)]
        turn += [((0, dx), q) for dx in (1, 3, 2) for q in (0, 1)]
        return turn + [((near, dx), part) for dx in (0, 1, 3, 2)]

    def z_link(near, part):
        turn = [(0, u) for u in range(4)] + [(near, 2 * part), (near, 2 * part + 1)]
        return turn + [(0, u) for u in range(4, 8)] + [(near, 4 + 2 * part), (near, 5 + 2 * part)]

    a_links = ((XA, x_link(3, 0)), (YA, y_link(3, 0)), (XB, x_link(1, 1)), (YB, y_link(1, 1)))
    z_links = ((1, z_link(3, 0)), (3, z_link(1, 1)))
    flying = {}

    def pace(link):
        queue = flying.setdefault(link, [])
        if len(queue) == DEPTH:
            queue.pop(0).wait_send()
        return queue

    def turn(k):
        for i, ((ly, lx), order) in enumerate(a_links):
            (dy, dx), q = order[k]
            queue = pace(i)
            a_wait(dy, dx, q)
            src = a_ref.at[pl.ds(2 * q, 2)] if (dy, dx) == (0, 0) else a_block(dy, dx, q)
            there = (dy ^ ly, dx ^ lx)
            queue.append(send(
                src, a_block(*there, q), a_send.at[i * 15 + k],
                a_recv.at[(there[0] * 4 + there[1]) * 4 + q],
                (((y ^ ly) << 2) | (x ^ lx), col), False,
            ))
        if k < 12:
            for i, (lz, order) in enumerate(z_links):
                dz, u = order[k]
                queue = pace(4 + i)
                f_wait(dz, u)
                src = f_ref.at[pl.ds(2 * u, 2)] if dz == 0 else f_block(dz, 0, u)
                queue.append(send(
                    src, f_block(dz, 0, u), f_send.at[i * 12 + k],
                    f_recv.at[(dz ^ lz) * 8 + u], (row, f_source(lz, 0)), False,
                ))

    def own_rows():
        for copy in scalars:
            copy.wait()
        lane = lax.broadcasted_iota(jnp.int32, (8, 128), 1)
        own_b, own_m = jnp.zeros((8, 128), jnp.int32), jnp.zeros((8, 128), jnp.int32)
        for s in range(16):
            value = jnp.where(s < count_ref[0, 0], cell_ref[0, s] + 1, 0)
            own_b = jnp.where(lane == col * 16 + s, value, own_b)
        for s in range(8):
            value = jnp.where(mlive_ref[0, s] > 0, mcol_ref[0, s] + 1, 0)
            own_m = jnp.where(lane == row * 8 + s, value, own_m)
        mb[0] = own_b
        mm[0] = own_m

    def m_exchange(k):
        if k < 4:
            send(mm.at[k], mm_in.at[k], m_send.at[k], m_recv.at[k], (row ^ NEAR_ROW[k], col))
        if k < 3:
            send(mb.at[k], mb_in.at[k], m_send.at[4 + k], m_recv.at[4 + k], (row, col ^ NEAR_COL[k]))

    def m_add(k):
        if k < 4:
            arrived(mm_in.at[k], m_recv.at[k])
            mm[k + 1] = mm[k] + mm_in[k]
        if k < 3:
            arrived(mb_in.at[k], m_recv.at[4 + k])
            mb[k + 1] = mb[k] + mb_in[k]

    s_ref[BLANK] = jnp.zeros((TILE, TILE), jnp.float32)

    def group_of(n):
        dy, q = ORDER[n]
        return groups[dy * 2 + q], ((y ^ dy) << 1) | ((x >> 1) ^ q)

    def add_product(o, f_tile, a_tile, gain):
        before = s_ref[tab[1, o]]
        after = jnp.dot(f_tile, a_tile, preferred_element_type=jnp.float32) + before
        s_ref[o] = after
        more = (jnp.minimum(1.0, after) - jnp.minimum(1.0, before)).reshape(8, TILE // 8, TILE)
        return gain + jnp.where(tab[3, o] > 0, jnp.sum(more, axis=0), 0.0)

    def products(n, gain):
        a_group, source = group_of(n)
        for dx in (0, 1):
            a_wait(ORDER[n][0], 2 * ORDER[n][1] + dx, 0, 1, 2, 3)

        def lower(s, gain):
            o = n * 8 + s
            return add_product(o, fl[source * 8 + s], a_group[tab[0, o]], gain)

        gain = lax.fori_loop(0, 8, lower, gain, unroll=UNROLL)

        def upper(j, carry):
            tile = a_group[tab[0, LOWER + j]]
            if n == 0:
                picked[j] = tile
            else:
                picked[j] = jnp.where(tab[5, LOWER + j] == source, tile, picked[j])
            return carry

        if n < 7:
            lax.fori_loop(0, 8, upper, 0)
        return gain

    total = jnp.zeros((TILE // 8, TILE), jnp.float32)
    for k in range(15):
        turn(k)
        if k == 0:
            own_rows()
            m_exchange(0)
        if k in (1, 3, 5):
            m_add(k // 2)
            m_exchange(k // 2 + 1)
        if k == 2:
            sib_send(0, 0, 1, 2, 3)
        if k == 6:
            sib_send(1, 0, 1)
            sib_send(3, 0, 1)
        if k == 7:
            m_add(3)
            tables(tab_v, mb[3, 0:1, :], mm[4, 0:1, :], y, x, col)
            to_scalars = pltpu.make_async_copy(tab_v, tab, local_sem.at[4])
            to_scalars.start()
            to_scalars.wait()
        if k == 8:
            sib_send(2, 0, 1)
            for e in (1, 2, 3):
                pl.semaphore_signal(plane_sem, inc=1, device_id=(row, col ^ (2 * e)), device_id_type=MESH)
        if k == 10:
            for copy in local:
                copy.wait()
            sib_wait(0)

            def widen(s, carry):
                s_ref[PRODUCTS + s] = fl[col * 8 + s].astype(jnp.float32)
                s_ref[PRODUCTS + 8 + s] = fu[col * 8 + s].astype(jnp.float32)
                return carry

            lax.fori_loop(0, 8, widen, 0)
            total = products(0, total)
        if k == 11:
            total = products(1, total)
            total = products(2, total)
        if k == 12:
            pl.semaphore_wait(plane_sem, 3)
            sib_send(1, 2, 3)
            sib_send(3, 2, 3)
        if k == 13:
            total = products(3, total)
    sib_send(2, 2, 3)
    for n in range(4, 8):
        total = products(n, total)
    sib_wait(1)

    def spilled(j, gain):
        o = LOWER + j
        a_group, source = group_of(7)
        tile = jnp.where(tab[5, o] == source, a_group[tab[0, o]], picked[j])
        return add_product(o, fu[tab[4, o]], tile, gain)

    total = lax.fori_loop(0, 8, spilled, total, unroll=UNROLL)

    def output(c, carry):
        for i in range(2):
            out_ref[pl.ds(i * TILE, TILE), pl.ds(pl.multiple_of(c * TILE, TILE), TILE)] = jnp.minimum(
                1.0, s_ref[tab[2, i * 16 + c]]
            ).astype(jnp.bfloat16)
        return carry

    total = jnp.sum(total.reshape(TILE // 64, 8, TILE), axis=0)
    pair[0] = total[:, :128] + total[:, 128:]
    send(pair.at[0], pair.at[1], g_send.at[0], g_recv.at[0], (row, col ^ 1))
    lax.fori_loop(0, 6, output, 0)
    arrived(pair.at[1], g_recv.at[0])
    gains[0] = pair[0] + pair[1]
    me = (z << 4) | row

    def to_chip(n, carry):
        @pl.when(n != me)
        def _():
            to_row, to_z = n & 15, n >> 4
            pltpu.make_async_remote_copy(
                src_ref=gains.at[0], dst_ref=gains.at[((row ^ to_row) << 2) | (z ^ to_z)],
                send_sem=g_send.at[1], recv_sem=g_recv.at[1],
                device_id=(to_row, (to_z << 1) | core), device_id_type=MESH,
            ).start()

        return carry

    lax.fori_loop(0, CHIPS, to_chip, 0, unroll=4)
    lax.fori_loop(6, 16, output, 0)
    for queue in flying.values():
        started.extend(queue)
    for copy in started:
        copy.wait_send()
    others = gains.at[pl.ds(1, CHIPS - 1)]
    arrived(others, g_recv.at[1])
    part = gains[...]
    while part.shape[0] > 1:
        part = part.reshape(part.shape[0] // 2, 2, 8, 128)
        part = part[:, 0] + part[:, 1]
    rest = jnp.concatenate([part[0], jnp.zeros((8, 128), jnp.float32)])
    for k in range(3):
        piece = rest.astype(jnp.bfloat16)
        out_ref[pl.ds(2 * TILE, 16), pl.ds(k * 128, 128)] = piece
        rest = rest - piece.astype(jnp.float32)
    pltpu.make_async_remote_copy(
        src_ref=others, dst_ref=others, send_sem=g_send.at[1], recv_sem=g_recv.at[1],
        device_id=(row ^ 1, col), device_id_type=MESH,
    ).wait_send()


def store_kernel(from_ref, to_ref, gain_ref, gain_s, sem):
    rows = [pl.ds(128 * i, 128) for i in range(4)]
    copies = [pltpu.make_async_copy(from_ref.at[r], to_ref.at[r], sem.at[i]) for i, r in enumerate(rows)]
    for copy in copies:
        copy.start()
    gain = jnp.zeros((16, 128), jnp.float32)
    for k in (2, 1, 0):
        gain += from_ref[pl.ds(2 * TILE, 16), pl.ds(k * 128, 128)].astype(jnp.float32)
    gain_s[0, 0] = jnp.sum(gain) * (1.0 / 268435456.0)
    copies.append(pltpu.make_async_copy(gain_s, gain_ref, sem.at[4]))
    copies[-1].start()
    for copy in copies:
        copy.wait()


def on_device(band_tiles, band_cell, band_count, matrix_tiles, matrix_col, matrix_live):
    vmem = pl.BlockSpec(memory_space=pltpu.VMEM)
    hbm = pl.BlockSpec(memory_space=pl.ANY)
    tiles = (TILE, TILE)
    both = pl.pallas_call(
        kernel,
        out_shape=pltpu.VMEM((2 * TILE + 16, 16 * TILE), jnp.bfloat16),
        in_specs=[hbm] * 6,
        out_specs=vmem,
        scratch_shapes=[pltpu.SMEM((1, n), jnp.int32) for n in (16, 1, 8, 8)]
        + [pltpu.VMEM((16, *tiles), jnp.bfloat16)] * 8
        + [
            pltpu.VMEM((LOWER, *tiles), jnp.bfloat16),
            pltpu.VMEM((LOWER, *tiles), jnp.bfloat16),
            pltpu.VMEM((BLANK + 1, *tiles), jnp.float32),
            pltpu.VMEM((8, *tiles), jnp.bfloat16),
            pltpu.VMEM((4, 8, 128), jnp.int32),
            pltpu.VMEM((5, 8, 128), jnp.int32),
            pltpu.VMEM((3, 8, 128), jnp.int32),
            pltpu.VMEM((4, 8, 128), jnp.int32),
            pltpu.VMEM((8, 128), jnp.int32),
            pltpu.SMEM((8, 128), jnp.int32),
            pltpu.VMEM((2, 8, 128), jnp.float32),
            pltpu.VMEM((64, 8, 128), jnp.float32),
            pltpu.SemaphoreType.DMA((60,)),
            pltpu.SemaphoreType.DMA((64,)),
            pltpu.SemaphoreType.DMA((40,)),
            pltpu.SemaphoreType.DMA((48,)),
            pltpu.SemaphoreType.DMA((7,)),
            pltpu.SemaphoreType.DMA((7,)),
            pltpu.SemaphoreType.DMA((2,)),
            pltpu.SemaphoreType.DMA((2,)),
            pltpu.SemaphoreType.REGULAR,
            pltpu.SemaphoreType.DMA((9,)),
        ],
        compiler_params=pltpu.CompilerParams(
            collective_id=0, has_side_effects=True, vmem_limit_bytes=57 * 1024 * 1024
        ),
    )(band_cell, band_count, matrix_col, matrix_live, band_tiles[0], matrix_tiles[0])
    reached, gain = pl.pallas_call(
        store_kernel,
        out_shape=(
            jax.ShapeDtypeStruct((2 * TILE, 16 * TILE), jnp.bfloat16),
            jax.ShapeDtypeStruct((1, 1), jnp.float32),
        ),
        in_specs=[vmem],
        out_specs=(hbm, hbm),
        scratch_shapes=[pltpu.SMEM((1, 1), jnp.float32), pltpu.SemaphoreType.DMA((5,))],
        compiler_params=pltpu.CompilerParams(vmem_limit_bytes=1024 * 1024),
    )(pltpu.with_memory_space_constraint(both, pltpu.VMEM))
    return reached, gain.reshape(())


def solution(mesh):
    placed = P("row", "col")
    tiled = P("row", "col", None, None)
    return jax.shard_map(
        on_device, mesh=mesh,
        in_specs=(tiled, placed, placed, tiled, placed, placed),
        out_specs=(placed, P()), check_vma=False,
    )
```

```python
import functools

import jax
import jax.numpy as jnp
from jax import lax
from jax.experimental import pallas as pl
from jax.experimental.pallas import tpu as pltpu
from jax.sharding import PartitionSpec as P

TILE = 256
N_ROW, N_COL = 16, 8
SPOTS = 32
LOWER = 64
PRODUCTS = 72
BLANK = PRODUCTS + 16
ORDER = ((0, 0), (1, 0), (3, 0), (0, 1), (1, 1), (2, 0), (3, 1), (2, 1))
UNROLL = 8
DEPTH = 2
XA, XB, YA, YB = (0, 1), (0, 3), (1, 0), (3, 0)
NEAR_ROW, NEAR_COL = (1, 3, 4, 12), (2, 6, 1)
CHIPS = 64
MESH = pl.DeviceIdType.MESH


def tables(tab_v, enc_row, menc_row, y, x, col):
    shape = (128, 128)
    r = lax.broadcasted_iota(jnp.int32, shape, 0)
    l = lax.broadcasted_iota(jnp.int32, shape, 1)
    r1 = lax.broadcasted_iota(jnp.int32, (128, 1), 0)
    zero = jnp.zeros(shape, jnp.int32)
    eye = r == l

    def lanes(v):
        return jnp.sum(v, axis=1, keepdims=True)

    def to_row(column):
        return jnp.sum(jnp.where(eye, column + zero, 0), axis=0, keepdims=True)

    enc = enc_row + zero
    enc_col = lanes(jnp.where(eye, enc, 0))
    up_col = jnp.where(enc_col > 0, 1, 0) * ((r1 >> 3) & 1)
    rank_row = jnp.sum(jnp.where(r < l, up_col + zero, 0), axis=0, keepdims=True)
    up = jnp.where(enc > 0, 1, 0) * ((l >> 3) & 1)
    group = r1 >> 3
    source = jnp.zeros((128, 1), jnp.int32)
    for n, (dy, q) in enumerate(ORDER):
        source = jnp.where(group == n, ((y ^ dy) << 1) | ((x >> 1) ^ q), source)
    slot = (source << 4) + (r1 & 7)
    low_hit = jnp.where(l == slot + zero, 1, 0)
    up_hit = up * jnp.where(rank_row + zero == r - LOWER, 1, 0)
    pick = jnp.where(r < LOWER, low_hit, up_hit)
    cell_col = lanes(pick * enc)
    t_col = lanes(pick * l)
    cell = jnp.maximum(cell_col - 1, 0)
    kk, src = cell & 15, t_col >> 4
    menc_col = lanes(jnp.where(l == ((src << 4) + kk) + zero, menc_row + zero, 0))
    good = jnp.where(cell_col > 0, 1, 0) * jnp.where(menc_col > 0, 1, 0)
    pos_col = jnp.where(good > 0, ((cell >> 4) << 4) + menc_col - 1, -1)
    pos = pos_col + zero
    pos_row = to_row(pos_col)
    same = jnp.where(pos == pos_row + zero, 1, 0) * jnp.where(pos >= 0, 1, 0) * jnp.where(r < l, 1, 0)
    prev = jnp.max(jnp.where(same > 0, r, -1), axis=0, keepdims=True)
    last = jnp.max(jnp.where(pos == l, r, -1), axis=0, keepdims=True)
    own = jnp.where((r1 >> 4) == col, 1, 0)
    own_at = own * jnp.where(enc_col > 0, 1, 0)
    base = jnp.max(jnp.where((own_at * enc_col + zero) == l + 1, r & 15, -1), axis=0, keepdims=True)
    base = jnp.where(base < 0, BLANK, PRODUCTS + base)
    base_col = lanes(jnp.where(pos == l, base + zero, 0))
    base_of = to_row(jnp.where(pos_col < 0, BLANK, base_col))
    a_index = (((kk >> 3) ^ (x & 1)) << 3) | (kk & 7)
    tab_v[0:1, :] = to_row(a_index)
    tab_v[1:2, :] = jnp.where(prev < 0, base_of, prev)
    tab_v[2:3, :] = jnp.where(last < 0, base, last)
    tab_v[3:4, :] = to_row(good)
    tab_v[4:5, :] = to_row(((t_col >> 4) << 3) + (t_col & 7))
    tab_v[5:6, :] = to_row(src)
    tab_v[6:8, :] = jnp.zeros((2, 128), jnp.int32)


def kernel(
    cell_in, count_in, mcol_in, mlive_in, f_ref, a_ref, out_ref,
    cell_ref, count_ref, mcol_ref, mlive_ref,
    a0, a1, a2, a3, a4, a5, a6, a7, fl, fu, s_ref, picked, mb, mm, mb_in, mm_in, tab_v, tab, pair, gains,
    a_send, a_recv, f_send, f_recv, m_send, m_recv, g_send, g_recv, plane_sem, local_sem,
):
    row, col = lax.axis_index("row"), lax.axis_index("col")
    y, x, z, core = row >> 2, row & 3, col >> 1, col & 1
    groups = (a0, a1, a2, a3, a4, a5, a6, a7)

    barrier = pltpu.get_barrier_semaphore()
    for d in NEAR_ROW:
        pl.semaphore_signal(barrier, inc=1, device_id=(row ^ d, col), device_id_type=MESH)
    for d in NEAR_COL:
        pl.semaphore_signal(barrier, inc=1, device_id=(row, col ^ d), device_id_type=MESH)

    scalars = [
        pltpu.make_async_copy(there, here, local_sem.at[5 + i])
        for i, (there, here) in enumerate(
            ((cell_in, cell_ref), (count_in, count_ref), (mcol_in, mcol_ref), (mlive_in, mlive_ref))
        )
    ]
    for copy in scalars:
        copy.start()
    local = [
        pltpu.make_async_copy(a_ref, a0.at[pl.ds(0, 8)], local_sem.at[0]),
        pltpu.make_async_copy(f_ref.at[pl.ds(0, 8)], fl.at[pl.ds(col * 8, 8)], local_sem.at[1]),
        pltpu.make_async_copy(f_ref.at[pl.ds(8, 8)], fu.at[pl.ds(col * 8, 8)], local_sem.at[2]),
    ]
    for copy in local:
        copy.start()

    pl.semaphore_wait(barrier, len(NEAR_ROW) + len(NEAR_COL))

    started = []

    def send(src, dst, send_sem, recv_sem, device, keep=True):
        copy = pltpu.make_async_remote_copy(
            src_ref=src, dst_ref=dst, send_sem=send_sem, recv_sem=recv_sem,
            device_id=device, device_id_type=MESH,
        )
        copy.start()
        if keep:
            started.append(copy)
        return copy

    def arrived(ref, sem):
        pltpu.make_async_remote_copy(
            src_ref=ref, dst_ref=ref, send_sem=m_send.at[0], recv_sem=sem,
            device_id=(row ^ 1, col), device_id_type=MESH,
        ).wait_recv()

    def a_block(dy, dx, q):
        return groups[dy * 2 + (dx >> 1)].at[pl.ds((dx & 1) * 8 + 2 * q, 2)]

    a_here, f_here = set(), set()

    def a_wait(dy, dx, *quarters):
        for q in quarters:
            if (dy, dx) != (0, 0) and (dy, dx, q) not in a_here:
                a_here.add((dy, dx, q))
                arrived(a_block(dy, dx, q), a_recv.at[(dy * 4 + dx) * 4 + q])

    def f_source(dz, dc):
        return ((z ^ dz) << 1) | (core ^ dc)

    def f_block(dz, dc, u, n=2):
        upper, first = u // 4, 2 * (u % 4)
        return (fu if upper else fl).at[pl.ds(f_source(dz, dc) * 8 + first, n)]

    def f_wait(dz, *units):
        for u in units:
            if dz and (dz, u) not in f_here:
                f_here.add((dz, u))
                arrived(f_block(dz, 0, u), f_recv.at[dz * 8 + u])

    def sib_wait(upper):
        for dz in range(4):
            for u in (4 * upper, 4 * upper + 2):
                arrived(f_block(dz, 1, u, 4), f_recv.at[32 + dz * 4 + u // 2])

    def sib_send(dz, *halves):
        for h in halves:
            f_wait(dz, 2 * h, 2 * h + 1)
            src = f_ref.at[pl.ds(4 * h, 4)] if dz == 0 else f_block(dz, 0, 2 * h, 4)
            send(
                src, f_block(dz, 0, 2 * h, 4), f_send.at[24 + dz * 4 + h],
                f_recv.at[32 + dz * 4 + h], (row, col ^ 1),
            )

    def x_link(near, part):
        turn = [((0, 0), 0), ((0, 0), 1), ((0, 0), 2), ((0, near), part), ((0, 0), 3)]
        turn += [((dy, 0), q) for dy in (1, 3, 2) for q in (2, 3)]
        return turn + [((dy, near), part + 2) for dy in (0, 1, 3, 2)]

    def y_link(near, part):
        turn = [((0, 0), 2), ((0, 0), 3), ((0, 0), 0), ((near, 0), part + 2), ((0, 0), 1)]
        turn += [((0, dx), q) for dx in (1, 3, 2) for q in (0, 1)]
        return turn + [((near, dx), part) for dx in (0, 1, 3, 2)]

    def z_link(near, part):
        turn = [(0, u) for u in range(4)] + [(near, 2 * part), (near, 2 * part + 1)]
        return turn + [(0, u) for u in range(4, 8)] + [(near, 4 + 2 * part), (near, 5 + 2 * part)]

    a_links = ((XA, x_link(3, 0)), (YA, y_link(3, 0)), (XB, x_link(1, 1)), (YB, y_link(1, 1)))
    z_links = ((1, z_link(3, 0)), (3, z_link(1, 1)))
    flying = {}

    def pace(link):
        queue = flying.setdefault(link, [])
        if len(queue) == DEPTH:
            queue.pop(0).wait_send()
        return queue

    def turn(k):
        for i, ((ly, lx), order) in enumerate(a_links):
            (dy, dx), q = order[k]
            queue = pace(i)
            a_wait(dy, dx, q)
            src = a_ref.at[pl.ds(2 * q, 2)] if (dy, dx) == (0, 0) else a_block(dy, dx, q)
            there = (dy ^ ly, dx ^ lx)
            queue.append(send(
                src, a_block(*there, q), a_send.at[i * 15 + k],
                a_recv.at[(there[0] * 4 + there[1]) * 4 + q],
                (((y ^ ly) << 2) | (x ^ lx), col), False,
            ))
        if k < 12:
            for i, (lz, order) in enumerate(z_links):
                dz, u = order[k]
                queue = pace(4 + i)
                f_wait(dz, u)
                src = f_ref.at[pl.ds(2 * u, 2)] if dz == 0 else f_block(dz, 0, u)
                queue.append(send(
                    src, f_block(dz, 0, u), f_send.at[i * 12 + k],
                    f_recv.at[(dz ^ lz) * 8 + u], (row, f_source(lz, 0)), False,
                ))

    def own_rows():
        for copy in scalars:
            copy.wait()
        lane = lax.broadcasted_iota(jnp.int32, (8, 128), 1)
        own_b, own_m = jnp.zeros((8, 128), jnp.int32), jnp.zeros((8, 128), jnp.int32)
        for s in range(16):
            value = jnp.where(s < count_ref[0, 0], cell_ref[0, s] + 1, 0)
            own_b = jnp.where(lane == col * 16 + s, value, own_b)
        for s in range(8):
            value = jnp.where(mlive_ref[0, s] > 0, mcol_ref[0, s] + 1, 0)
            own_m = jnp.where(lane == row * 8 + s, value, own_m)
        mb[0] = own_b
        mm[0] = own_m

    def m_exchange(k):
        if k < 4:
            send(mm.at[k], mm_in.at[k], m_send.at[k], m_recv.at[k], (row ^ NEAR_ROW[k], col))
        if k < 3:
            send(mb.at[k], mb_in.at[k], m_send.at[4 + k], m_recv.at[4 + k], (row, col ^ NEAR_COL[k]))

    def m_add(k):
        if k < 4:
            arrived(mm_in.at[k], m_recv.at[k])
            mm[k + 1] = mm[k] + mm_in[k]
        if k < 3:
            arrived(mb_in.at[k], m_recv.at[4 + k])
            mb[k + 1] = mb[k] + mb_in[k]

    s_ref[BLANK] = jnp.zeros((TILE, TILE), jnp.float32)

    def group_of(n):
        dy, q = ORDER[n]
        return groups[dy * 2 + q], ((y ^ dy) << 1) | ((x >> 1) ^ q)

    def add_product(o, f_tile, a_tile, gain):
        before = s_ref[tab[1, o]]
        after = jnp.dot(f_tile, a_tile, preferred_element_type=jnp.float32) + before
        s_ref[o] = after
        more = (jnp.minimum(1.0, after) - jnp.minimum(1.0, before)).reshape(8, TILE // 8, TILE)
        return gain + jnp.where(tab[3, o] > 0, jnp.sum(more, axis=0), 0.0)

    def products(n, gain):
        a_group, source = group_of(n)
        for dx in (0, 1):
            a_wait(ORDER[n][0], 2 * ORDER[n][1] + dx, 0, 1, 2, 3)

        def lower(s, gain):
            o = n * 8 + s
            return add_product(o, fl[source * 8 + s], a_group[tab[0, o]], gain)

        gain = lax.fori_loop(0, 8, lower, gain, unroll=UNROLL)

        def upper(j, carry):
            tile = a_group[tab[0, LOWER + j]]
            if n == 0:
                picked[j] = tile
            else:
                picked[j] = jnp.where(tab[5, LOWER + j] == source, tile, picked[j])
            return carry

        if n < 7:
            lax.fori_loop(0, 8, upper, 0)
        return gain

    total = jnp.zeros((TILE // 8, TILE), jnp.float32)
    for k in range(15):
        turn(k)
        if k == 0:
            own_rows()
            m_exchange(0)
        if k in (1, 3, 5):
            m_add(k // 2)
            m_exchange(k // 2 + 1)
        if k == 2:
            sib_send(0, 0, 1, 2, 3)
        if k == 6:
            sib_send(1, 0, 1)
            sib_send(3, 0, 1)
        if k == 7:
            m_add(3)
            tables(tab_v, mb[3, 0:1, :], mm[4, 0:1, :], y, x, col)
            to_scalars = pltpu.make_async_copy(tab_v, tab, local_sem.at[4])
            to_scalars.start()
            to_scalars.wait()
        if k == 8:
            sib_send(2, 0, 1)
            for e in (1, 2, 3):
                pl.semaphore_signal(plane_sem, inc=1, device_id=(row, col ^ (2 * e)), device_id_type=MESH)
        if k == 10:
            for copy in local:
                copy.wait()
            sib_wait(0)

            def widen(s, carry):
                s_ref[PRODUCTS + s] = fl[col * 8 + s].astype(jnp.float32)
                s_ref[PRODUCTS + 8 + s] = fu[col * 8 + s].astype(jnp.float32)
                return carry

            lax.fori_loop(0, 8, widen, 0)
            total = products(0, total)
        if k == 11:
            total = products(1, total)
            total = products(2, total)
        if k == 12:
            pl.semaphore_wait(plane_sem, 3)
            sib_send(1, 2, 3)
            sib_send(3, 2, 3)
        if k == 13:
            total = products(3, total)
    sib_send(2, 2, 3)
    for n in range(4, 8):
        total = products(n, total)
    sib_wait(1)

    def spilled(j, gain):
        o = LOWER + j
        a_group, source = group_of(7)
        tile = jnp.where(tab[5, o] == source, a_group[tab[0, o]], picked[j])
        return add_product(o, fu[tab[4, o]], tile, gain)

    total = lax.fori_loop(0, 8, spilled, total, unroll=UNROLL)

    def output(c, carry):
        for i in range(2):
            out_ref[pl.ds(i * TILE, TILE), pl.ds(pl.multiple_of(c * TILE, TILE), TILE)] = jnp.minimum(
                1.0, s_ref[tab[2, i * 16 + c]]
            ).astype(jnp.bfloat16)
        return carry

    total = jnp.sum(total.reshape(TILE // 64, 8, TILE), axis=0)
    pair[0] = total[:, :128] + total[:, 128:]
    send(pair.at[0], pair.at[1], g_send.at[0], g_recv.at[0], (row, col ^ 1))
    lax.fori_loop(0, 3, output, 0)
    arrived(pair.at[1], g_recv.at[0])
    gains[0] = pair[0] + pair[1]
    me = (z << 4) | row

    def to_chip(n, carry):
        @pl.when(n != me)
        def _():
            to_row, to_z = n & 15, n >> 4
            pltpu.make_async_remote_copy(
                src_ref=gains.at[0], dst_ref=gains.at[((row ^ to_row) << 2) | (z ^ to_z)],
                send_sem=g_send.at[1], recv_sem=g_recv.at[1],
                device_id=(to_row, (to_z << 1) | core), device_id_type=MESH,
            ).start()

        return carry

    lax.fori_loop(0, CHIPS, to_chip, 0, unroll=4)
    lax.fori_loop(3, 16, output, 0)
    for queue in flying.values():
        started.extend(queue)
    for copy in started:
        copy.wait_send()
    others = gains.at[pl.ds(1, CHIPS - 1)]
    arrived(others, g_recv.at[1])
    part = gains[...]
    while part.shape[0] > 1:
        part = part.reshape(part.shape[0] // 2, 2, 8, 128)
        part = part[:, 0] + part[:, 1]
    rest = jnp.concatenate([part[0], jnp.zeros((8, 128), jnp.float32)])
    for k in range(3):
        piece = rest.astype(jnp.bfloat16)
        out_ref[pl.ds(2 * TILE, 16), pl.ds(k * 128, 128)] = piece
        rest = rest - piece.astype(jnp.float32)
    pltpu.make_async_remote_copy(
        src_ref=others, dst_ref=others, send_sem=g_send.at[1], recv_sem=g_recv.at[1],
        device_id=(row ^ 1, col), device_id_type=MESH,
    ).wait_send()


def store_kernel(from_ref, to_ref, gain_ref, gain_s, sem):
    rows = [pl.ds(128 * i, 128) for i in range(4)]
    copies = [pltpu.make_async_copy(from_ref.at[r], to_ref.at[r], sem.at[i]) for i, r in enumerate(rows)]
    for copy in copies:
        copy.start()
    gain = jnp.zeros((16, 128), jnp.float32)
    for k in (2, 1, 0):
        gain += from_ref[pl.ds(2 * TILE, 16), pl.ds(k * 128, 128)].astype(jnp.float32)
    gain_s[0, 0] = jnp.sum(gain) * (1.0 / 268435456.0)
    copies.append(pltpu.make_async_copy(gain_s, gain_ref, sem.at[4]))
    copies[-1].start()
    for copy in copies:
        copy.wait()


def on_device(band_tiles, band_cell, band_count, matrix_tiles, matrix_col, matrix_live):
    vmem = pl.BlockSpec(memory_space=pltpu.VMEM)
    hbm = pl.BlockSpec(memory_space=pl.ANY)
    tiles = (TILE, TILE)
    both = pl.pallas_call(
        kernel,
        out_shape=pltpu.VMEM((2 * TILE + 16, 16 * TILE), jnp.bfloat16),
        in_specs=[hbm] * 6,
        out_specs=vmem,
        scratch_shapes=[pltpu.SMEM((1, n), jnp.int32) for n in (16, 1, 8, 8)]
        + [pltpu.VMEM((16, *tiles), jnp.bfloat16)] * 8
        + [
            pltpu.VMEM((LOWER, *tiles), jnp.bfloat16),
            pltpu.VMEM((LOWER, *tiles), jnp.bfloat16),
            pltpu.VMEM((BLANK + 1, *tiles), jnp.float32),
            pltpu.VMEM((8, *tiles), jnp.bfloat16),
            pltpu.VMEM((4, 8, 128), jnp.int32),
            pltpu.VMEM((5, 8, 128), jnp.int32),
            pltpu.VMEM((3, 8, 128), jnp.int32),
            pltpu.VMEM((4, 8, 128), jnp.int32),
            pltpu.VMEM((8, 128), jnp.int32),
            pltpu.SMEM((8, 128), jnp.int32),
            pltpu.VMEM((2, 8, 128), jnp.float32),
            pltpu.VMEM((64, 8, 128), jnp.float32),
            pltpu.SemaphoreType.DMA((60,)),
            pltpu.SemaphoreType.DMA((64,)),
            pltpu.SemaphoreType.DMA((40,)),
            pltpu.SemaphoreType.DMA((48,)),
            pltpu.SemaphoreType.DMA((7,)),
            pltpu.SemaphoreType.DMA((7,)),
            pltpu.SemaphoreType.DMA((2,)),
            pltpu.SemaphoreType.DMA((2,)),
            pltpu.SemaphoreType.REGULAR,
            pltpu.SemaphoreType.DMA((9,)),
        ],
        compiler_params=pltpu.CompilerParams(
            collective_id=0, has_side_effects=True, vmem_limit_bytes=57 * 1024 * 1024
        ),
    )(band_cell, band_count, matrix_col, matrix_live, band_tiles[0], matrix_tiles[0])
    reached, gain = pl.pallas_call(
        store_kernel,
        out_shape=(
            jax.ShapeDtypeStruct((2 * TILE, 16 * TILE), jnp.bfloat16),
            jax.ShapeDtypeStruct((1, 1), jnp.float32),
        ),
        in_specs=[vmem],
        out_specs=(hbm, hbm),
        scratch_shapes=[pltpu.SMEM((1, 1), jnp.float32), pltpu.SemaphoreType.DMA((5,))],
        compiler_params=pltpu.CompilerParams(vmem_limit_bytes=1024 * 1024),
    )(pltpu.with_memory_space_constraint(both, pltpu.VMEM))
    return reached, gain.reshape(())


def solution(mesh):
    placed = P("row", "col")
    tiled = P("row", "col", None, None)
    return jax.shard_map(
        on_device, mesh=mesh,
        in_specs=(tiled, placed, placed, tiled, placed, placed),
        out_specs=(placed, P()), check_vma=False,
    )
```

```python
import functools

import jax
import jax.numpy as jnp
from jax import lax
from jax.experimental import pallas as pl
from jax.experimental.pallas import tpu as pltpu
from jax.sharding import PartitionSpec as P

TILE = 256
N_ROW, N_COL = 16, 8
SPOTS = 32
LOWER = 64
PRODUCTS = 72
BLANK = PRODUCTS + 16
ORDER = ((0, 0), (1, 0), (3, 0), (0, 1), (1, 1), (2, 0), (3, 1), (2, 1))
UNROLL = 8
DEPTH = 2
XA, XB, YA, YB = (0, 1), (0, 3), (1, 0), (3, 0)
NEAR_ROW, NEAR_COL = (1, 3, 4, 12), (2, 6, 1)
CHIPS = 64
MESH = pl.DeviceIdType.MESH


def tables(tab_v, enc_row, menc_row, y, x, col):
    shape = (128, 128)
    r = lax.broadcasted_iota(jnp.int32, shape, 0)
    l = lax.broadcasted_iota(jnp.int32, shape, 1)
    r1 = lax.broadcasted_iota(jnp.int32, (128, 1), 0)
    zero = jnp.zeros(shape, jnp.int32)
    eye = r == l

    def lanes(v):
        return jnp.sum(v, axis=1, keepdims=True)

    def to_row(column):
        return jnp.sum(jnp.where(eye, column + zero, 0), axis=0, keepdims=True)

    enc = enc_row + zero
    enc_col = lanes(jnp.where(eye, enc, 0))
    up_col = jnp.where(enc_col > 0, 1, 0) * ((r1 >> 3) & 1)
    rank_row = jnp.sum(jnp.where(r < l, up_col + zero, 0), axis=0, keepdims=True)
    up = jnp.where(enc > 0, 1, 0) * ((l >> 3) & 1)
    group = r1 >> 3
    source = jnp.zeros((128, 1), jnp.int32)
    for n, (dy, q) in enumerate(ORDER):
        source = jnp.where(group == n, ((y ^ dy) << 1) | ((x >> 1) ^ q), source)
    slot = (source << 4) + (r1 & 7)
    low_hit = jnp.where(l == slot + zero, 1, 0)
    up_hit = up * jnp.where(rank_row + zero == r - LOWER, 1, 0)
    pick = jnp.where(r < LOWER, low_hit, up_hit)
    cell_col = lanes(pick * enc)
    t_col = lanes(pick * l)
    cell = jnp.maximum(cell_col - 1, 0)
    kk, src = cell & 15, t_col >> 4
    menc_col = lanes(jnp.where(l == ((src << 4) + kk) + zero, menc_row + zero, 0))
    good = jnp.where(cell_col > 0, 1, 0) * jnp.where(menc_col > 0, 1, 0)
    pos_col = jnp.where(good > 0, ((cell >> 4) << 4) + menc_col - 1, -1)
    pos = pos_col + zero
    pos_row = to_row(pos_col)
    same = jnp.where(pos == pos_row + zero, 1, 0) * jnp.where(pos >= 0, 1, 0) * jnp.where(r < l, 1, 0)
    prev = jnp.max(jnp.where(same > 0, r, -1), axis=0, keepdims=True)
    last = jnp.max(jnp.where(pos == l, r, -1), axis=0, keepdims=True)
    own = jnp.where((r1 >> 4) == col, 1, 0)
    own_at = own * jnp.where(enc_col > 0, 1, 0)
    base = jnp.max(jnp.where((own_at * enc_col + zero) == l + 1, r & 15, -1), axis=0, keepdims=True)
    base = jnp.where(base < 0, BLANK, PRODUCTS + base)
    base_col = lanes(jnp.where(pos == l, base + zero, 0))
    base_of = to_row(jnp.where(pos_col < 0, BLANK, base_col))
    a_index = (((kk >> 3) ^ (x & 1)) << 3) | (kk & 7)
    tab_v[0:1, :] = to_row(a_index)
    tab_v[1:2, :] = jnp.where(prev < 0, base_of, prev)
    tab_v[2:3, :] = jnp.where(last < 0, base, last)
    tab_v[3:4, :] = to_row(good)
    tab_v[4:5, :] = to_row(((t_col >> 4) << 3) + (t_col & 7))
    tab_v[5:6, :] = to_row(src)
    tab_v[6:8, :] = jnp.zeros((2, 128), jnp.int32)


def kernel(
    cell_in, count_in, mcol_in, mlive_in, f_ref, a_ref, out_ref,
    cell_ref, count_ref, mcol_ref, mlive_ref,
    a0, a1, a2, a3, a4, a5, a6, a7, fl, fu, s_ref, picked, mb, mm, mb_in, mm_in, tab_v, tab, pair, gains,
    a_send, a_recv, f_send, f_recv, m_send, m_recv, g_send, g_recv, plane_sem, local_sem,
):
    row, col = lax.axis_index("row"), lax.axis_index("col")
    y, x, z, core = row >> 2, row & 3, col >> 1, col & 1
    groups = (a0, a1, a2, a3, a4, a5, a6, a7)

    barrier = pltpu.get_barrier_semaphore()
    for d in NEAR_ROW:
        pl.semaphore_signal(barrier, inc=1, device_id=(row ^ d, col), device_id_type=MESH)
    for d in NEAR_COL:
        pl.semaphore_signal(barrier, inc=1, device_id=(row, col ^ d), device_id_type=MESH)

    scalars = [
        pltpu.make_async_copy(there, here, local_sem.at[5 + i])
        for i, (there, here) in enumerate(
            ((cell_in, cell_ref), (count_in, count_ref), (mcol_in, mcol_ref), (mlive_in, mlive_ref))
        )
    ]
    for copy in scalars:
        copy.start()
    local = [
        pltpu.make_async_copy(a_ref, a0.at[pl.ds(0, 8)], local_sem.at[0]),
        pltpu.make_async_copy(f_ref.at[pl.ds(0, 8)], fl.at[pl.ds(col * 8, 8)], local_sem.at[1]),
        pltpu.make_async_copy(f_ref.at[pl.ds(8, 8)], fu.at[pl.ds(col * 8, 8)], local_sem.at[2]),
    ]
    for copy in local:
        copy.start()

    pl.semaphore_wait(barrier, len(NEAR_ROW) + len(NEAR_COL))

    started = []

    def send(src, dst, send_sem, recv_sem, device, keep=True):
        copy = pltpu.make_async_remote_copy(
            src_ref=src, dst_ref=dst, send_sem=send_sem, recv_sem=recv_sem,
            device_id=device, device_id_type=MESH,
        )
        copy.start()
        if keep:
            started.append(copy)
        return copy

    def arrived(ref, sem):
        pltpu.make_async_remote_copy(
            src_ref=ref, dst_ref=ref, send_sem=m_send.at[0], recv_sem=sem,
            device_id=(row ^ 1, col), device_id_type=MESH,
        ).wait_recv()

    def a_block(dy, dx, q):
        return groups[dy * 2 + (dx >> 1)].at[pl.ds((dx & 1) * 8 + 2 * q, 2)]

    a_here, f_here = set(), set()

    def a_wait(dy, dx, *quarters):
        for q in quarters:
            if (dy, dx) != (0, 0) and (dy, dx, q) not in a_here:
                a_here.add((dy, dx, q))
                arrived(a_block(dy, dx, q), a_recv.at[(dy * 4 + dx) * 4 + q])

    def f_source(dz, dc):
        return ((z ^ dz) << 1) | (core ^ dc)

    def f_block(dz, dc, u, n=2):
        upper, first = u // 4, 2 * (u % 4)
        return (fu if upper else fl).at[pl.ds(f_source(dz, dc) * 8 + first, n)]

    def f_wait(dz, *units):
        for u in units:
            if dz and (dz, u) not in f_here:
                f_here.add((dz, u))
                arrived(f_block(dz, 0, u), f_recv.at[dz * 8 + u])

    def sib_wait(upper):
        for dz in range(4):
            for u in (4 * upper, 4 * upper + 2):
                arrived(f_block(dz, 1, u, 4), f_recv.at[32 + dz * 4 + u // 2])

    def sib_send(dz, *halves):
        for h in halves:
            f_wait(dz, 2 * h, 2 * h + 1)
            src = f_ref.at[pl.ds(4 * h, 4)] if dz == 0 else f_block(dz, 0, 2 * h, 4)
            send(
                src, f_block(dz, 0, 2 * h, 4), f_send.at[24 + dz * 4 + h],
                f_recv.at[32 + dz * 4 + h], (row, col ^ 1),
            )

    def x_link(near, part):
        turn = [((0, 0), 0), ((0, 0), 1), ((0, 0), 2), ((0, near), part), ((0, 0), 3)]
        turn += [((dy, 0), q) for dy in (1, 3, 2) for q in (2, 3)]
        return turn + [((dy, near), part + 2) for dy in (0, 1, 3, 2)]

    def y_link(near, part):
        turn = [((0, 0), 2), ((0, 0), 3), ((0, 0), 0), ((near, 0), part + 2), ((0, 0), 1)]
        turn += [((0, dx), q) for dx in (1, 3, 2) for q in (0, 1)]
        return turn + [((near, dx), part) for dx in (0, 1, 3, 2)]

    def z_link(near, part):
        turn = [(0, u) for u in range(4)] + [(near, 2 * part), (near, 2 * part + 1)]
        return turn + [(0, u) for u in range(4, 8)] + [(near, 4 + 2 * part), (near, 5 + 2 * part)]

    a_links = ((XA, x_link(3, 0)), (YA, y_link(3, 0)), (XB, x_link(1, 1)), (YB, y_link(1, 1)))
    z_links = ((1, z_link(3, 0)), (3, z_link(1, 1)))
    flying = {}

    def pace(link):
        queue = flying.setdefault(link, [])
        if len(queue) == DEPTH:
            queue.pop(0).wait_send()
        return queue

    def turn(k):
        for i, ((ly, lx), order) in enumerate(a_links):
            (dy, dx), q = order[k]
            queue = pace(i)
            a_wait(dy, dx, q)
            src = a_ref.at[pl.ds(2 * q, 2)] if (dy, dx) == (0, 0) else a_block(dy, dx, q)
            there = (dy ^ ly, dx ^ lx)
            queue.append(send(
                src, a_block(*there, q), a_send.at[i * 15 + k],
                a_recv.at[(there[0] * 4 + there[1]) * 4 + q],
                (((y ^ ly) << 2) | (x ^ lx), col), False,
            ))
        if k < 12:
            for i, (lz, order) in enumerate(z_links):
                dz, u = order[k]
                queue = pace(4 + i)
                f_wait(dz, u)
                src = f_ref.at[pl.ds(2 * u, 2)] if dz == 0 else f_block(dz, 0, u)
                queue.append(send(
                    src, f_block(dz, 0, u), f_send.at[i * 12 + k],
                    f_recv.at[(dz ^ lz) * 8 + u], (row, f_source(lz, 0)), False,
                ))

    def own_rows():
        for copy in scalars:
            copy.wait()
        lane = lax.broadcasted_iota(jnp.int32, (8, 128), 1)
        own_b, own_m = jnp.zeros((8, 128), jnp.int32), jnp.zeros((8, 128), jnp.int32)
        for s in range(16):
            value = jnp.where(s < count_ref[0, 0], cell_ref[0, s] + 1, 0)
            own_b = jnp.where(lane == col * 16 + s, value, own_b)
        for s in range(8):
            value = jnp.where(mlive_ref[0, s] > 0, mcol_ref[0, s] + 1, 0)
            own_m = jnp.where(lane == row * 8 + s, value, own_m)
        mb[0] = own_b
        mm[0] = own_m

    def m_exchange(k):
        if k < 4:
            send(mm.at[k], mm_in.at[k], m_send.at[k], m_recv.at[k], (row ^ NEAR_ROW[k], col))
        if k < 3:
            send(mb.at[k], mb_in.at[k], m_send.at[4 + k], m_recv.at[4 + k], (row, col ^ NEAR_COL[k]))

    def m_add(k):
        if k < 4:
            arrived(mm_in.at[k], m_recv.at[k])
            mm[k + 1] = mm[k] + mm_in[k]
        if k < 3:
            arrived(mb_in.at[k], m_recv.at[4 + k])
            mb[k + 1] = mb[k] + mb_in[k]

    s_ref[BLANK] = jnp.zeros((TILE, TILE), jnp.float32)

    def group_of(n):
        dy, q = ORDER[n]
        return groups[dy * 2 + q], ((y ^ dy) << 1) | ((x >> 1) ^ q)

    def add_product(o, f_tile, a_tile, gain):
        before = s_ref[tab[1, o]]
        after = jnp.dot(f_tile, a_tile, preferred_element_type=jnp.float32) + before
        s_ref[o] = after
        more = (jnp.minimum(1.0, after) - jnp.minimum(1.0, before)).reshape(8, TILE // 8, TILE)
        return gain + jnp.where(tab[3, o] > 0, jnp.sum(more, axis=0), 0.0)

    def products(n, gain):
        a_group, source = group_of(n)
        for dx in (0, 1):
            a_wait(ORDER[n][0], 2 * ORDER[n][1] + dx, 0, 1, 2, 3)

        def lower(s, gain):
            o = n * 8 + s
            return add_product(o, fl[source * 8 + s], a_group[tab[0, o]], gain)

        gain = lax.fori_loop(0, 8, lower, gain, unroll=UNROLL)

        def upper(j, carry):
            tile = a_group[tab[0, LOWER + j]]
            if n == 0:
                picked[j] = tile
            else:
                picked[j] = jnp.where(tab[5, LOWER + j] == source, tile, picked[j])
            return carry

        if n < 7:
            lax.fori_loop(0, 8, upper, 0)
        return gain

    total = jnp.zeros((TILE // 8, TILE), jnp.float32)
    for k in range(15):
        turn(k)
        if k == 0:
            own_rows()
            m_exchange(0)
        if k in (1, 3, 5):
            m_add(k // 2)
            m_exchange(k // 2 + 1)
        if k == 2:
            sib_send(0, 0, 1, 2, 3)
        if k == 6:
            sib_send(1, 0, 1)
            sib_send(3, 0, 1)
        if k == 7:
            m_add(3)
            tables(tab_v, mb[3, 0:1, :], mm[4, 0:1, :], y, x, col)
            to_scalars = pltpu.make_async_copy(tab_v, tab, local_sem.at[4])
            to_scalars.start()
            to_scalars.wait()
        if k == 8:
            sib_send(2, 0, 1)
            for e in (1, 2, 3):
                pl.semaphore_signal(plane_sem, inc=1, device_id=(row, col ^ (2 * e)), device_id_type=MESH)
        if k == 10:
            for copy in local:
                copy.wait()
            sib_wait(0)

            def widen(s, carry):
                s_ref[PRODUCTS + s] = fl[col * 8 + s].astype(jnp.float32)
                s_ref[PRODUCTS + 8 + s] = fu[col * 8 + s].astype(jnp.float32)
                return carry

            lax.fori_loop(0, 8, widen, 0)
            total = products(0, total)
        if k == 11:
            total = products(1, total)
            total = products(2, total)
        if k == 12:
            pl.semaphore_wait(plane_sem, 3)
            sib_send(1, 2, 3)
            sib_send(3, 2, 3)
        if k == 13:
            total = products(3, total)
    sib_send(2, 2, 3)
    for n in range(4, 7):
        total = products(n, total)
    sib_wait(1)
    total = products(7, total)

    def spilled(j, gain):
        o = LOWER + j
        a_group, source = group_of(7)
        tile = jnp.where(tab[5, o] == source, a_group[tab[0, o]], picked[j])
        return add_product(o, fu[tab[4, o]], tile, gain)

    total = lax.fori_loop(0, 8, spilled, total, unroll=UNROLL)

    def output(c, carry):
        for i in range(2):
            out_ref[pl.ds(i * TILE, TILE), pl.ds(pl.multiple_of(c * TILE, TILE), TILE)] = jnp.minimum(
                1.0, s_ref[tab[2, i * 16 + c]]
            ).astype(jnp.bfloat16)
        return carry

    total = jnp.sum(total.reshape(TILE // 64, 8, TILE), axis=0)
    pair[0] = total[:, :128] + total[:, 128:]
    send(pair.at[0], pair.at[1], g_send.at[0], g_recv.at[0], (row, col ^ 1))
    lax.fori_loop(0, 6, output, 0)
    arrived(pair.at[1], g_recv.at[0])
    gains[0] = pair[0] + pair[1]
    me = (z << 4) | row

    def to_chip(n, carry):
        @pl.when(n != me)
        def _():
            to_row, to_z = n & 15, n >> 4
            pltpu.make_async_remote_copy(
                src_ref=gains.at[0], dst_ref=gains.at[((row ^ to_row) << 2) | (z ^ to_z)],
                send_sem=g_send.at[1], recv_sem=g_recv.at[1],
                device_id=(to_row, (to_z << 1) | core), device_id_type=MESH,
            ).start()

        return carry

    lax.fori_loop(0, CHIPS, to_chip, 0, unroll=4)
    lax.fori_loop(6, 16, output, 0)
    for queue in flying.values():
        started.extend(queue)
    for copy in started:
        copy.wait_send()
    others = gains.at[pl.ds(1, CHIPS - 1)]
    arrived(others, g_recv.at[1])
    part = gains[...]
    while part.shape[0] > 1:
        part = part.reshape(part.shape[0] // 2, 2, 8, 128)
        part = part[:, 0] + part[:, 1]
    rest = jnp.concatenate([part[0], jnp.zeros((8, 128), jnp.float32)])
    for k in range(3):
        piece = rest.astype(jnp.bfloat16)
        out_ref[pl.ds(2 * TILE, 16), pl.ds(k * 128, 128)] = piece
        rest = rest - piece.astype(jnp.float32)
    pltpu.make_async_remote_copy(
        src_ref=others, dst_ref=others, send_sem=g_send.at[1], recv_sem=g_recv.at[1],
        device_id=(row ^ 1, col), device_id_type=MESH,
    ).wait_send()


def store_kernel(from_ref, to_ref, gain_ref, gain_s, sem):
    rows = [pl.ds(128 * i, 128) for i in range(4)]
    copies = [pltpu.make_async_copy(from_ref.at[r], to_ref.at[r], sem.at[i]) for i, r in enumerate(rows)]
    for copy in copies:
        copy.start()
    gain = jnp.zeros((16, 128), jnp.float32)
    for k in (2, 1, 0):
        gain += from_ref[pl.ds(2 * TILE, 16), pl.ds(k * 128, 128)].astype(jnp.float32)
    gain_s[0, 0] = jnp.sum(gain) * (1.0 / 268435456.0)
    copies.append(pltpu.make_async_copy(gain_s, gain_ref, sem.at[4]))
    copies[-1].start()
    for copy in copies:
        copy.wait()


def on_device(band_tiles, band_cell, band_count, matrix_tiles, matrix_col, matrix_live):
    vmem = pl.BlockSpec(memory_space=pltpu.VMEM)
    hbm = pl.BlockSpec(memory_space=pl.ANY)
    tiles = (TILE, TILE)
    both = pl.pallas_call(
        kernel,
        out_shape=pltpu.VMEM((2 * TILE + 16, 16 * TILE), jnp.bfloat16),
        in_specs=[hbm] * 6,
        out_specs=vmem,
        scratch_shapes=[pltpu.SMEM((1, n), jnp.int32) for n in (16, 1, 8, 8)]
        + [pltpu.VMEM((16, *tiles), jnp.bfloat16)] * 8
        + [
            pltpu.VMEM((LOWER, *tiles), jnp.bfloat16),
            pltpu.VMEM((LOWER, *tiles), jnp.bfloat16),
            pltpu.VMEM((BLANK + 1, *tiles), jnp.float32),
            pltpu.VMEM((8, *tiles), jnp.bfloat16),
            pltpu.VMEM((4, 8, 128), jnp.int32),
            pltpu.VMEM((5, 8, 128), jnp.int32),
            pltpu.VMEM((3, 8, 128), jnp.int32),
            pltpu.VMEM((4, 8, 128), jnp.int32),
            pltpu.VMEM((8, 128), jnp.int32),
            pltpu.SMEM((8, 128), jnp.int32),
            pltpu.VMEM((2, 8, 128), jnp.float32),
            pltpu.VMEM((64, 8, 128), jnp.float32),
            pltpu.SemaphoreType.DMA((60,)),
            pltpu.SemaphoreType.DMA((64,)),
            pltpu.SemaphoreType.DMA((40,)),
            pltpu.SemaphoreType.DMA((48,)),
            pltpu.SemaphoreType.DMA((7,)),
            pltpu.SemaphoreType.DMA((7,)),
            pltpu.SemaphoreType.DMA((2,)),
            pltpu.SemaphoreType.DMA((2,)),
            pltpu.SemaphoreType.REGULAR,
            pltpu.SemaphoreType.DMA((9,)),
        ],
        compiler_params=pltpu.CompilerParams(
            collective_id=0, has_side_effects=True, vmem_limit_bytes=57 * 1024 * 1024
        ),
    )(band_cell, band_count, matrix_col, matrix_live, band_tiles[0], matrix_tiles[0])
    reached, gain = pl.pallas_call(
        store_kernel,
        out_shape=(
            jax.ShapeDtypeStruct((2 * TILE, 16 * TILE), jnp.bfloat16),
            jax.ShapeDtypeStruct((1, 1), jnp.float32),
        ),
        in_specs=[vmem],
        out_specs=(hbm, hbm),
        scratch_shapes=[pltpu.SMEM((1, 1), jnp.float32), pltpu.SemaphoreType.DMA((5,))],
        compiler_params=pltpu.CompilerParams(vmem_limit_bytes=1024 * 1024),
    )(pltpu.with_memory_space_constraint(both, pltpu.VMEM))
    return reached, gain.reshape(())


def solution(mesh):
    placed = P("row", "col")
    tiled = P("row", "col", None, None)
    return jax.shard_map(
        on_device, mesh=mesh,
        in_specs=(tiled, placed, placed, tiled, placed, placed),
        out_specs=(placed, P()), check_vma=False,
    )
```
